256 devices in a mesh: pb: 16 (over z_hi, y, core), ma: 16 (over z_lo, x).
Axes of the slice: x: 4, y: 4, z: 8 (z_hi: 2, z_lo: 4; z = z_hi * 4 + z_lo), core: 2. Of those that a mesh axis runs over, the one named last changes fastest.
Arguments:
- queries: bfloat16 [16384, 4096], P('pb', 'ma'), may hold values from -6 to 6
- keys: bfloat16 [4096, 4096], P('ma', 'pb'), may hold values from -6 to 6
- query_ids: int32 [16384], P('pb'), may hold values from 0 to 31999, as said below
- memory_ids: int32 [4096], P('ma'), may hold values from 0 to 31999, as said below
- target_gap: float32 [16384], P('pb'), may hold values from -4 to -0.5
- lse: float32 [16384], P('pb'), as said below
- counts: int32 [16384], P('pb'), may hold values from 1 to 8
Outputs:
- query_grad: float32 [16384, 4096], P('pb', 'ma')
- key_grad: float32 [4096, 4096], P('ma', 'pb')
The draws below stay inside these ranges and needn't reach their ends.
Inputs may be any that keep to these rules, and one draw needn't show every extreme that they name: query_ids and memory_ids are token ids drawn from one common frequency law, so that some query and memory rows share tokens. query_ids follow the same law as memory_ids. lse lies between log(4096) + 0.5 and log(4096) + 4.
All inputs are finite; a program needn't handle non-finite values.
Results may differ from the reference program's by a relative error of at most 0.0059.
Values may be sent and summed in bfloat16 or wider, within the bound.
A program may use at most 64 MiB of HBM per device.

```python
import math
import jax
import jax.numpy as jnp
from jax import lax

D = 4096
VOCAB = 32000
GRAD_SCALE = 1024
NQ = 16384
NM = 4096


def token_table(key, which, length):
    order = jax.random.permutation(jax.random.fold_in(key, 7001), VOCAB)
    uniform_bits = jax.random.randint(jax.random.fold_in(key, which), (length,), 0, 2 ** 20)
    ranks = 2 ** 24 // (uniform_bits + 2 ** 10) - 16
    return order[ranks % VOCAB].astype(jnp.int32)


def draw_query_ids(key, part):
    return token_table(key, 11, NQ)


def draw_memory_ids(key, part):
    return token_table(key, 23, NM)


def draw_lse(key, part):
    inner = jax.random.fold_in(key, 31)
    spread = jax.random.uniform(inner, (NQ,), jnp.float32, 1.0, 3.0)
    return spread + jnp.log(jnp.float32(NM))


def set_ends(array, stream_key, smallest, largest):
    index_at = [jax.random.randint(jax.random.fold_in(stream_key, axis), (), 0, length) for axis, length in enumerate(array.shape)]
    longest = array.shape.index(max(array.shape))
    beside = index_at[:longest] + [(index_at[longest] + 1) % array.shape[longest]] + index_at[longest + 1:]
    return array.at[tuple(index_at)].set(smallest).at[tuple(beside)].set(largest)


def level_of(rng, dims, shards, least, top_value):
    def one(axis_at, parts):
        heights = jax.random.uniform(jax.random.fold_in(jax.random.fold_in(rng, 6), axis_at), (parts,), jnp.float32, least / len(shards), top_value / len(shards))
        return jnp.repeat(jnp.exp(heights), dims[axis_at] // parts).reshape((-1,) + (1,) * (len(dims) - axis_at - 1))

    gain = one(*shards[0])
    for cut in shards[1:]:
        gain = gain * one(*cut)
    return gain


def gaussian(own_key, shape, scale, limit, shards=(), held_as=jnp.bfloat16):
    drawn = scale * jax.random.normal(own_key, shape, jnp.float32)
    if shards:
        drawn = drawn * level_of(own_key, shape, shards, -0.22, 0.18)
    return jnp.clip(drawn, -limit, limit).astype(held_as)


def setup_inputs(seed: int = 0) -> dict:
    seeds = jax.random.split(jax.random.key(seed), 8)
    return {
        "queries": gaussian(seeds[0], (NQ, D), 1.0, 6.0, ((0, 16), (1, 16))),
        "keys": gaussian(seeds[1], (NM, D), 1.0, 6.0, ((0, 16), (1, 16))),
        "query_ids": draw_query_ids(jax.random.fold_in(seeds[7], 71), 0),
        "memory_ids": draw_memory_ids(jax.random.fold_in(seeds[7], 71), 0),
        "target_gap": jnp.clip(-4.0 + 3.5 * jax.random.uniform(seeds[4], (NQ,), jnp.float32) ** level_of(seeds[4], (NQ,), ((0, 16),), -0.2, 0.2), -4.0, -0.5),
        "lse": draw_lse(jax.random.fold_in(seeds[7], 71), 0),
        "counts": set_ends(jax.random.randint(seeds[6], (NQ,), 1, 9), jax.random.fold_in(seeds[6], 1), 1, 8).astype(jnp.int32),
    }


def reference(queries, keys, query_ids, memory_ids, target_gap, lse, counts):
    factor = 1.0 / math.sqrt(D)
    scores = jnp.dot(queries, keys.T, preferred_element_type=jnp.float32) * factor
    prob = jnp.exp(scores - lse[:, None])
    match = (query_ids[:, None] == memory_ids[None, :]).astype(jnp.float32)
    positive = jnp.exp(target_gap) + lax.optimization_barrier(jnp.sum(match * prob, axis=1))
    row_scale = jnp.float32(GRAD_SCALE) / counts.astype(jnp.float32)
    weight = ((prob - match * prob / positive[:, None]) * row_scale[:, None]).astype(jnp.bfloat16)
    query_grad = jnp.dot(weight, keys, preferred_element_type=jnp.float32) * factor
    key_grad = jnp.dot(weight.T, queries, preferred_element_type=jnp.float32) * factor
    return (query_grad, key_grad)
```

```python
import math

import jax
import jax.numpy as jnp
from jax import lax
from jax.experimental import pallas as pl
from jax.experimental.pallas import tpu as pltpu
from jax.sharding import Mesh
from jax.sharding import PartitionSpec as P

D = 4096
GRAD_SCALE = 1024
AXES = ("zh", "y", "core", "zl", "x")
PB = ("zh", "y", "core")
MA = ("zl", "x")
FACTOR = 1.0 / math.sqrt(D)
BLK = 256
ZFIRST = 160
F32 = jnp.float32
BF16 = jnp.bfloat16
OFFSETS = (0, 1, -1, 2, -2, 3, -3, 4)
RANK = {dz: i for i, dz in enumerate(OFFSETS)}
N_SENDS = 200


def nt(a, b):
    return lax.dot_general(a, b, (((1,), (1,)), ((), ())), preferred_element_type=F32)


def nn(a, b):
    return jnp.dot(a, b, preferred_element_type=F32)


def kernel(
    q_ref, k_ref, qid_ref, mid_ref, gap_ref, lse_ref, cnt_ref, oq_ref, ok_ref,
    qb, kb, st, sx, idb, mb, wt, wn, dkp, yb, yb2, za, zb, dqp, rb, ab,
    ssem, s_kz, s_ky, s_bz, s_by, s_q, s_id, s_sx, s_m, s_w, s_y, s_y2, s_za, s_zb, s_r, s_a,
):
    zh, y, c, zl, x = [lax.axis_index(a) for a in AXES]
    z = zh * 4 + zl
    xp = lax.rem(x, 2)
    xs = x // 2
    home = xp == c
    oc = 1 - c
    a = ZFIRST
    ah = a // 2
    b = BLK - a
    bh = b // 2

    def zat(dz):
        return lax.rem(z + dz + 8, 8)

    def dev(dx=0, dy=0, dz=0, core=None, zl_to=None, x_to=None):
        zz = zat(dz)
        return (
            zz // 4,
            lax.rem(y + dy, 4),
            c if core is None else core,
            lax.rem(zz, 4) if zl_to is None else zl_to,
            lax.rem(x + dx, 4) if x_to is None else x_to,
        )

    def span(i, n=BLK):
        return pl.ds(pl.multiple_of(i * n, n), n)

    sends = []

    def send(src, dst, recv, to, when=None):
        copy = pltpu.make_async_remote_copy(
            src_ref=src,
            dst_ref=dst,
            send_sem=ssem.at[len(sends)],
            recv_sem=recv,
            device_id=to,
            device_id_type=pl.DeviceIdType.MESH,
        )
        if when is None:
            copy.start()
        else:
            pl.when(when)(copy.start)
        sends.append((copy, when))

    partner = dev(core=oc)

    def got(dst, recv):
        pltpu.make_async_remote_copy(
            src_ref=dst,
            dst_ref=dst,
            send_sem=ssem.at[0],
            recv_sem=recv,
            device_id=partner,
            device_id_type=pl.DeviceIdType.MESH,
        ).wait_recv()

    barrier = pltpu.get_barrier_semaphore()
    peers = [partner, dev(dz=1), dev(dz=-1)]
    for d in (1, 2, 3):
        other = lax.rem(zl + d, 4)
        peers += [dev(dx=d), dev(dy=d), dev(zl_to=other), dev(zl_to=other, core=oc)]
    for peer in peers:
        pl.semaphore_signal(barrier, inc=1, device_id=peer, device_id_type=pl.DeviceIdType.MESH)
    ycols = span(y)
    kb[z, :, ycols] = k_ref[...]
    idb[zl] = jnp.broadcast_to(mid_ref[...], (8, BLK))
    pl.semaphore_wait(barrier, len(peers))

    def zslot(dz):
        return kb.at[zat(dz)]

    def a_block(dz, dy, rows):
        return kb.at[zat(dz), rows, span(lax.rem(y + dy, 4))]

    def a_z(dz, step, rows, part):
        blk = a_block(dz, 0, rows)
        to = dz - step
        i = 8 if part == 1 else RANK[4 if to == -4 else to]
        send(blk, blk, s_kz.at[i], dev(dz=step))

    def a_y(dz):
        blk = a_block(dz, 0, pl.ds(0, a))
        for dy in (1, 3, 2):
            send(blk, blk, s_ky.at[RANK[dz], 3 - dy], dev(dy=dy))

    def a_arrive(dz):
        for sign in (-1, 1) if dz < 4 else (0,):
            if dz == 4:
                got(a_block(4, 0, pl.ds(0, ah)), s_kz.at[7])
                got(a_block(4, 0, pl.ds(ah, ah)), s_kz.at[8])
                a_y(4)
                continue
            at = sign * dz
            got(a_block(at, 0, pl.ds(0, a)), s_kz.at[RANK[at]])
            if dz < 3:
                a_z(at, -sign, pl.ds(0, a), 0)
            elif sign < 0:
                a_z(at, 1, pl.ds(0, ah), 0)
            else:
                a_z(at, -1, pl.ds(ah, ah), 1)
        if dz < 4:
            a_y(-dz)
            a_y(dz)

    def b_z(dz, step, rows, part):
        blk = kb.at[zat(dz), rows]
        to = dz - step
        i = 8 if part == 1 else RANK[4 if to == -4 else to]
        send(blk, blk, s_bz.at[i], dev(dz=step))

    def b_arrive(dz):
        for sign in (-1, 1):
            at = sign * dz
            got(kb.at[zat(at), pl.ds(a, b)], s_bz.at[RANK[at]])
            if dz < 3:
                b_z(at, -sign, pl.ds(a, b), 0)
            elif sign < 0:
                b_z(at, 1, pl.ds(a, bh), 0)
            else:
                b_z(at, -1, pl.ds(a + bh, bh), 1)

    def q_block(j, r):
        return qb.at[span(r), span(j)]

    j_own = zl * 2 + xs
    a_z(0, 1, pl.ds(0, a), 0)
    a_z(0, -1, pl.ds(0, a), 0)
    blk = a_block(0, 0, pl.ds(a, b))
    for dy in (1, 3, 2):
        send(blk, blk, s_by.at[3 - dy], dev(dy=dy))
    a_y(0)
    send(q_ref.at[span(zl)], q_block(j_own, c), s_q.at[j_own, c], dev(core=xp), when=jnp.logical_not(home))
    for d in (1, 3, 2):
        to = lax.rem(zl + d, 4)
        send(q_ref.at[span(to)], q_block(j_own, c), s_q.at[j_own, c], dev(zl_to=to, core=xp))
    for d in (1, 2, 3):
        send(idb.at[zl], idb.at[zl], s_id.at[3 - d], dev(zl_to=lax.rem(zl + d, 4)))

    @pl.when(home)
    def _():
        qb[span(c), span(j_own)] = q_ref[span(zl), :]

    def q_spread(j, r, wait):
        if wait:
            pl.when(home)(lambda: got(q_block(j, r), s_q.at[j, r]))
        for dx in (1, 3, 2):
            send(q_block(j, r), q_block(j, r), s_q.at[j, r], dev(dx=dx), when=home)

    def q_arrive(d):
        j = lax.rem(zl + d, 4) * 2 + xs
        q_spread(j, 0, True)
        q_spread(j, 1, True)

    q_spread(j_own, c, False)
    q_spread(j_own, oc, True)
    a_arrive(1)
    for dy in (1, 3, 2):
        got(a_block(0, 4 - dy, pl.ds(a, b)), s_by.at[3 - dy])
    b_z(0, 1, pl.ds(a, b), 0)
    b_z(0, -1, pl.ds(a, b), 0)
    q_arrive(1)
    a_arrive(2)
    q_arrive(3)
    a_arrive(3)
    b_arrive(1)
    q_arrive(2)
    a_arrive(4)
    b_arrive(2)
    b_arrive(3)

    for d in (1, 3, 2):
        other = lax.rem(zl + d, 4)
        got(idb.at[other], s_id.at[d - 1])
    for d in (0, 1, 3, 2):
        for r in (0, 1):
            j = lax.rem(zl + d, 4) * 2 + (1 - xs)
            got(q_block(j, r), s_q.at[j, r])

    @pl.when(jnp.logical_not(home))
    def _():
        for d in (0, 1, 3, 2):
            for r in (0, 1):
                j = lax.rem(zl + d, 4) * 2 + xs
                got(q_block(j, r), s_q.at[j, r])

    qrow = span(zl)
    qid = qid_ref[:, qrow].astype(F32)
    lse = lse_ref[:, qrow]

    def match_of(m):
        ids = jnp.broadcast_to(idb[m][0:1, :].astype(F32), (128, BLK)).T
        return ids[:, 0:1] == qid

    def scores(dz, last):
        i = RANK[dz]
        for dy in (1, 3, 2):
            got(a_block(dz, 4 - dy, pl.ds(0, a)), s_ky.at[i, 3 - dy])
        if dz == 4:
            got(kb.at[zat(4), pl.ds(a, bh)], s_bz.at[7])
            got(kb.at[zat(4), pl.ds(a + bh, bh)], s_bz.at[8])
        m = lax.rem(zat(dz), 4)
        part = zat(dz) // 4
        for r in (oc, c):
            s = nt(kb[zat(dz)], qb[span(r), span(part, 1024)])
            st[m, r] = st[m, r] + s if last else s
            if last and r is oc:
                send(st.at[m, oc], sx.at[m], s_sx.at[m], partner)

    def probs(dz):
        m = lax.rem(zat(dz), 4)
        got(sx.at[m], s_sx.at[m])
        p = jnp.exp((st[m, c] + sx[m]) * FACTOR - lse)
        st[m, c] = p
        return jnp.sum(jnp.where(match_of(m), p, 0.0), axis=0, keepdims=True)

    for dz in (0, 1, -1, 2):
        scores(dz, False)
    scores(-2, True)
    scores(3, True)
    matched = probs(-2)
    scores(-3, True)
    matched = matched + probs(3)
    scores(4, True)
    matched = matched + probs(-3)
    matched = matched + probs(4)

    mb[0] = jnp.broadcast_to(matched, (8, BLK))
    for d in (1, 3, 2):
        send(mb.at[0], mb.at[4 - d], s_m.at[3 - d], dev(dx=d))
    scale = jnp.float32(GRAD_SCALE) / cnt_ref[:, qrow].astype(F32)
    gap = jnp.exp(gap_ref[:, qrow])
    for d in (1, 3, 2):
        got(mb.at[4 - d], s_m.at[3 - d])
    positive = gap + ((mb[0] + mb[1]) + (mb[2] + mb[3]))[0:1, :]
    inverse = 1.0 / positive

    order = (0, 3, 1, 2)
    for d in order:
        m = lax.rem(zl + d, 4)
        p = st[m, c]
        w = (p - jnp.where(match_of(m), p * inverse, 0.0)) * scale
        wt[m, :, span(c)] = w.astype(BF16)
        blk = wt.at[m, :, span(c)]
        send(blk, blk, s_w.at[m], partner)
        wn[span(c), span(m)] = w.T.astype(BF16)
    for d in order:
        m = lax.rem(zl + d, 4)
        got(wt.at[m, :, span(oc)], s_w.at[m])
        wn[span(oc), span(m)] = wt[m, :, span(oc)].astype(F32).T.astype(BF16)

    def key_part(dz):
        i = RANK[dz]
        m = lax.rem(zat(dz), 4)
        part = zat(dz) // 4
        dkp[i] = (nn(wt[m], qb[:, span(part, 1024)]) * FACTOR).astype(BF16)
        for dy in (1, 3, 2):
            to = span(lax.rem(y + dy, 4))
            send(dkp.at[i, pl.ds(0, a), to], yb.at[i, 3 - dy], s_y.at[i, 3 - dy], dev(dy=dy))

    def chain(dz, buf, sem, half):
        way = 0 if dz > 0 else 1
        left = abs(dz)
        if left == 3:
            rows = pl.ds(0, half) if dz > 0 else pl.ds(half, half)
        else:
            rows = pl.ds(0, 2 * half)
        got(buf.at[way, left, rows], sem.at[way, left])
        return way, left, rows

    def a_sum(dz):
        i = RANK[dz]
        for s in range(3):
            got(yb.at[i, s], s_y.at[i, s])
        total = dkp[i, pl.ds(0, a), ycols].astype(F32) + yb[i, 0].astype(F32)
        return total + (yb[i, 1].astype(F32) + yb[i, 2].astype(F32))

    def a_pass(dz):
        i = RANK[dz]
        dkp[i, pl.ds(0, a), ycols] = a_sum(dz).astype(BF16)
        if dz == 4:
            for way, rows in ((0, pl.ds(0, ah)), (1, pl.ds(ah, ah))):
                send(dkp.at[i, rows, ycols], za.at[way, 3, rows], s_za.at[way, 3], dev(dz=1 - 2 * way))
            return
        way, left, rows = chain(dz, za, s_za, ah)
        mine = dkp[i, rows, ycols].astype(F32) + za[way, left, rows].astype(F32)
        dkp[i, rows, ycols] = mine.astype(BF16)
        send(dkp.at[i, pl.ds(0, a), ycols], za.at[way, left - 1], s_za.at[way, left - 1], dev(dz=1 - 2 * way))

    def b_pass(dz):
        i = RANK[dz]
        if dz == 4:
            for way, rows in ((0, 0), (1, bh)):
                src = dkp.at[i, pl.ds(a + rows, bh)]
                send(src, zb.at[way, 3, pl.ds(rows, bh)], s_zb.at[way, 3], dev(dz=1 - 2 * way))
            return
        way, left, rows = chain(dz, zb, s_zb, bh)
        mine = pl.ds(a + rows.start, rows.size)
        dkp[i, mine] = (dkp[i, mine].astype(F32) + zb[way, left, rows].astype(F32)).astype(BF16)
        send(dkp.at[i, pl.ds(a, b)], zb.at[way, left - 1], s_zb.at[way, left - 1], dev(dz=1 - 2 * way))

    def query_part(d, s):
        zf = lax.rem(zl + d, 4)
        j = zf * 2 + s
        keys = kb[pl.ds(pl.multiple_of((zf // 2) * 4, 4), 4), :, span(lax.rem(j, 4))]
        dqp[j] = (nn(wn[...], keys.reshape(1024, BLK)) * FACTOR).astype(BF16)
        to = 2 * s + c
        slot = lax.rem(x - to + 4, 4) - 1
        if s is xs:
            slot = jnp.maximum(slot, 0)
        send(
            dqp.at[j], rb.at[slot, zf], s_r.at[slot, zf], dev(x_to=to),
            when=jnp.logical_not(home) if s is xs else None,
        )

    def query_sum(d):
        zf = lax.rem(zl + d, 4)
        j = zf * 2 + xs

        @pl.when(home)
        def _():
            for s in range(3):
                got(rb.at[s, zf], s_r.at[s, zf])
            total = (dqp[j].astype(F32) + rb[0, zf].astype(F32)) + (
                rb[1, zf].astype(F32) + rb[2, zf].astype(F32)
            )
            dqp[j] = total.astype(BF16)
            if d == 0:
                oq_ref[span(zl), :] = dqp[j, span(c)].astype(F32)

        if d == 0:
            send(dqp.at[j, span(oc)], ab.at[zl], s_a.at[zl], partner, when=home)
        else:
            for r in (0, 1):
                send(dqp.at[j, span(r)], ab.at[zl], s_a.at[zl], dev(zl_to=zf, core=r), when=home)

    far = 1 - xs
    key_part(4)
    b_pass(4)
    key_part(3)
    key_part(-3)
    query_part(2, far)
    query_part(2, xs)
    key_part(2)
    key_part(-2)
    b_pass(3)
    b_pass(-3)
    query_part(1, far)
    query_part(1, xs)
    a_pass(4)
    query_part(3, far)
    query_part(3, xs)
    key_part(1)
    key_part(-1)
    b_pass(2)
    b_pass(-2)
    query_part(0, far)
    query_part(0, xs)
    key_part(0)
    a_pass(3)
    a_pass(-3)
    query_sum(2)
    b_pass(1)
    b_pass(-1)
    a_pass(2)
    a_pass(-2)
    query_sum(1)
    for way in (0, 1):
        got(zb.at[way, 0], s_zb.at[way, 0])
    rest = dkp[0, pl.ds(a, b)].astype(F32) + (zb[0, 0].astype(F32) + zb[1, 0].astype(F32))
    dkp[0, pl.ds(a, b)] = rest.astype(BF16)
    for dy in (1, 3, 2):
        to = span(lax.rem(y + dy, 4))
        send(dkp.at[0, pl.ds(a, b), to], yb2.at[3 - dy], s_y2.at[3 - dy], dev(dy=dy))
    query_sum(3)
    a_pass(1)
    a_pass(-1)
    query_sum(0)
    total = a_sum(0)
    for s in range(3):
        got(yb2.at[s], s_y2.at[s])
    ok_ref[pl.ds(a, b), :] = (dkp[0, pl.ds(a, b), ycols].astype(F32) + yb2[0].astype(F32)) + (
        yb2[1].astype(F32) + yb2[2].astype(F32)
    )
    for d in (2, 1, 3):
        src = lax.rem(zl + d, 4)
        got(ab.at[src], s_a.at[src])
        oq_ref[span(src), :] = ab[src].astype(F32)

    @pl.when(jnp.logical_not(home))
    def _():
        got(ab.at[zl], s_a.at[zl])
        oq_ref[span(zl), :] = ab[zl].astype(F32)

    for way in (0, 1):
        got(za.at[way, 0], s_za.at[way, 0])
    ok_ref[pl.ds(0, a), :] = total + (za[0, 0].astype(F32) + za[1, 0].astype(F32))

    for copy, when in sends:
        if when is None:
            copy.wait_send()
        else:
            pl.when(when)(copy.wait_send)


def on_device(queries, keys, query_ids, memory_ids, target_gap, lse, counts):
    a = ZFIRST
    b = BLK - a
    vmem = pl.BlockSpec(memory_space=pltpu.VMEM)
    dma = pltpu.SemaphoreType.DMA
    return pl.pallas_call(
        kernel,
        out_shape=(
            jax.ShapeDtypeStruct((1024, BLK), F32),
            jax.ShapeDtypeStruct((BLK, BLK), F32),
        ),
        in_specs=[vmem] * 7,
        out_specs=(vmem, vmem),
        scratch_shapes=[
            pltpu.VMEM((512, 2048), BF16),
            pltpu.VMEM((8, BLK, 1024), BF16),
            pltpu.VMEM((4, 2, BLK, BLK), F32),
            pltpu.VMEM((4, BLK, BLK), F32),
            pltpu.VMEM((4, 8, BLK), jnp.int32),
            pltpu.VMEM((4, 8, BLK), F32),
            pltpu.VMEM((4, BLK, 512), BF16),
            pltpu.VMEM((512, 1024), BF16),
            pltpu.VMEM((8, BLK, 1024), BF16),
            pltpu.VMEM((8, 3, a, BLK), BF16),
            pltpu.VMEM((3, b, BLK), BF16),
            pltpu.VMEM((2, 4, a, BLK), BF16),
            pltpu.VMEM((2, 4, b, 1024), BF16),
            pltpu.VMEM((8, 512, BLK), BF16),
            pltpu.VMEM((3, 4, 512, BLK), BF16),
            pltpu.VMEM((4, BLK, BLK), BF16),
            dma((N_SENDS,)),
            dma((9,)),
            dma((8, 3)),
            dma((9,)),
            dma((3,)),
            dma((8, 2)),
            dma((3,)),
            dma((4,)),
            dma((3,)),
            dma((4,)),
            dma((8, 3)),
            dma((3,)),
            dma((2, 4)),
            dma((2, 4)),
            dma((3, 4)),
            dma((4,)),
        ],
        compiler_params=pltpu.CompilerParams(
            collective_id=0, has_side_effects=True, vmem_limit_bytes=56 * 2**20
        ),
        cost_estimate=pl.CostEstimate(
            flops=6_442_450_944, bytes_accessed=3_000_000, transcendentals=262_144
        ),
        name="contrastive_backward",
    )(
        queries,
        keys,
        query_ids.reshape(1, -1),
        memory_ids.reshape(1, -1),
        target_gap.reshape(1, -1),
        lse.reshape(1, -1),
        counts.reshape(1, -1),
    )


def solution(mesh):
    torus = Mesh(mesh.devices.reshape(2, 4, 2, 4, 4), AXES)
    return jax.shard_map(
        on_device,
        mesh=torus,
        in_specs=(P(PB, MA), P(MA, PB), P(PB), P(MA), P(PB), P(PB), P(PB)),
        out_specs=(P(PB, MA), P(MA, PB)),
        check_vma=False,
    )
```

```python
import math

import jax
import jax.numpy as jnp
from jax import lax
from jax.experimental import pallas as pl
from jax.experimental.pallas import tpu as pltpu
from jax.sharding import Mesh
from jax.sharding import PartitionSpec as P

D = 4096
GRAD_SCALE = 1024
AXES = ("zh", "y", "core", "zl", "x")
PB = ("zh", "y", "core")
MA = ("zl", "x")
FACTOR = 1.0 / math.sqrt(D)
BLK = 256
ZFIRST = 192
F32 = jnp.float32
BF16 = jnp.bfloat16
OFFSETS = (0, 1, -1, 2, -2, 3, -3, 4)
RANK = {dz: i for i, dz in enumerate(OFFSETS)}
N_SENDS = 200


def nt(a, b):
    return lax.dot_general(a, b, (((1,), (1,)), ((), ())), preferred_element_type=F32)


def nn(a, b):
    return jnp.dot(a, b, preferred_element_type=F32)


def kernel(
    q_ref, k_ref, qid_ref, mid_ref, gap_ref, lse_ref, cnt_ref, oq_ref, ok_ref,
    qb, kb, st, sx, idb, mb, wt, wn, dkp, yb, yb2, za, zb, dqp, rb, ab,
    ssem, s_kz, s_ky, s_bz, s_by, s_q, s_id, s_sx, s_m, s_w, s_y, s_y2, s_za, s_zb, s_r, s_a,
):
    zh, y, c, zl, x = [lax.axis_index(a) for a in AXES]
    z = zh * 4 + zl
    xp = lax.rem(x, 2)
    xs = x // 2
    home = xp == c
    oc = 1 - c
    a = ZFIRST
    ah = a // 2
    b = BLK - a
    bh = b // 2

    def zat(dz):
        return lax.rem(z + dz + 8, 8)

    def dev(dx=0, dy=0, dz=0, core=None, zl_to=None, x_to=None):
        zz = zat(dz)
        return (
            zz // 4,
            lax.rem(y + dy, 4),
            c if core is None else core,
            lax.rem(zz, 4) if zl_to is None else zl_to,
            lax.rem(x + dx, 4) if x_to is None else x_to,
        )

    def span(i, n=BLK):
        return pl.ds(pl.multiple_of(i * n, n), n)

    sends = []

    def send(src, dst, recv, to, when=None):
        copy = pltpu.make_async_remote_copy(
            src_ref=src,
            dst_ref=dst,
            send_sem=ssem.at[len(sends)],
            recv_sem=recv,
            device_id=to,
            device_id_type=pl.DeviceIdType.MESH,
        )
        if when is None:
            copy.start()
        else:
            pl.when(when)(copy.start)
        sends.append((copy, when))

    partner = dev(core=oc)

    def got(dst, recv):
        pltpu.make_async_remote_copy(
            src_ref=dst,
            dst_ref=dst,
            send_sem=ssem.at[0],
            recv_sem=recv,
            device_id=partner,
            device_id_type=pl.DeviceIdType.MESH,
        ).wait_recv()

    barrier = pltpu.get_barrier_semaphore()
    peers = [partner, dev(dz=1), dev(dz=-1)]
    for d in (1, 2, 3):
        other = lax.rem(zl + d, 4)
        peers += [dev(dx=d), dev(dy=d), dev(zl_to=other), dev(zl_to=other, core=oc)]
    for peer in peers:
        pl.semaphore_signal(barrier, inc=1, device_id=peer, device_id_type=pl.DeviceIdType.MESH)
    ycols = span(y)
    kb[z, :, ycols] = k_ref[...]
    idb[zl] = jnp.broadcast_to(mid_ref[...], (8, BLK))
    pl.semaphore_wait(barrier, len(peers))

    def zslot(dz):
        return kb.at[zat(dz)]

    def a_block(dz, dy, rows):
        return kb.at[zat(dz), rows, span(lax.rem(y + dy, 4))]

    def a_z(dz, step, rows, part):
        blk = a_block(dz, 0, rows)
        to = dz - step
        i = 8 if part == 1 else RANK[4 if to == -4 else to]
        send(blk, blk, s_kz.at[i], dev(dz=step))

    def a_y(dz):
        blk = a_block(dz, 0, pl.ds(0, a))
        for dy in (1, 3):
            send(blk, blk, s_ky.at[RANK[dz], 3 - dy], dev(dy=dy))

    def a_relay(*offsets):
        for dz in offsets:
            i = RANK[dz]
            got(a_block(dz, 3, pl.ds(0, a)), s_ky.at[i, 2])
            blk = a_block(dz, 3, pl.ds(0, ah))
            send(blk, blk, s_ky.at[i, 1], dev(dy=1))
            got(a_block(dz, 1, pl.ds(0, a)), s_ky.at[i, 0])
            blk = a_block(dz, 1, pl.ds(ah, ah))
            send(blk, blk, s_ky.at[i, 3], dev(dy=3))

    def a_arrive(dz):
        for sign in (-1, 1) if dz < 4 else (0,):
            if dz == 4:
                got(a_block(4, 0, pl.ds(0, ah)), s_kz.at[7])
                got(a_block(4, 0, pl.ds(ah, ah)), s_kz.at[8])
                a_y(4)
                continue
            at = sign * dz
            got(a_block(at, 0, pl.ds(0, a)), s_kz.at[RANK[at]])
            if dz < 3:
                a_z(at, -sign, pl.ds(0, a), 0)
            elif sign < 0:
                a_z(at, 1, pl.ds(0, ah), 0)
            else:
                a_z(at, -1, pl.ds(ah, ah), 1)
        if dz < 4:
            a_y(-dz)
            a_y(dz)

    def b_z(dz, step, rows, part):
        blk = kb.at[zat(dz), rows]
        to = dz - step
        i = 8 if part == 1 else RANK[4 if to == -4 else to]
        send(blk, blk, s_bz.at[i], dev(dz=step))

    def b_arrive(dz):
        for sign in (-1, 1):
            at = sign * dz
            got(kb.at[zat(at), pl.ds(a, b)], s_bz.at[RANK[at]])
            if dz < 3:
                b_z(at, -sign, pl.ds(a, b), 0)
            elif sign < 0:
                b_z(at, 1, pl.ds(a, bh), 0)
            else:
                b_z(at, -1, pl.ds(a + bh, bh), 1)

    def q_block(j, r):
        return qb.at[span(r), span(j)]

    j_own = zl * 2 + xs
    for d in (1, 2, 3):
        send(idb.at[zl], idb.at[zl], s_id.at[3 - d], dev(zl_to=lax.rem(zl + d, 4)))
    send(q_ref.at[span(zl)], q_block(j_own, c), s_q.at[j_own, c], dev(core=xp), when=jnp.logical_not(home))
    a_z(0, 1, pl.ds(0, a), 0)
    a_z(0, -1, pl.ds(0, a), 0)
    for d in (1, 3, 2):
        to = lax.rem(zl + d, 4)
        send(q_ref.at[span(to)], q_block(j_own, c), s_q.at[j_own, c], dev(zl_to=to, core=xp))
    blk = a_block(0, 0, pl.ds(a, b))
    for dy in (1, 3, 2):
        send(blk, blk, s_by.at[3 - dy], dev(dy=dy))
    a_y(0)

    @pl.when(home)
    def _():
        qb[span(c), span(j_own)] = q_ref[span(zl), :]

    def q_spread(j, r, wait):
        if wait:
            pl.when(home)(lambda: got(q_block(j, r), s_q.at[j, r]))
        for dx in (1, 3, 2):
            send(q_block(j, r), q_block(j, r), s_q.at[j, r], dev(dx=dx), when=home)

    def q_arrive(d):
        j = lax.rem(zl + d, 4) * 2 + xs
        q_spread(j, 0, True)
        q_spread(j, 1, True)

    q_spread(j_own, c, False)
    q_spread(j_own, oc, True)
    a_arrive(1)
    for dy in (1, 3, 2):
        got(a_block(0, 4 - dy, pl.ds(a, b)), s_by.at[3 - dy])
    b_z(0, 1, pl.ds(a, b), 0)
    b_z(0, -1, pl.ds(a, b), 0)
    a_relay(0)
    q_arrive(1)
    a_arrive(2)
    b_arrive(1)
    a_relay(1)
    q_arrive(3)
    a_arrive(3)
    a_relay(-1)
    b_arrive(2)
    q_arrive(2)
    a_arrive(4)
    a_relay(2)
    b_arrive(3)
    a_relay(-2, 3, -3, 4)

    for d in (1, 3, 2):
        other = lax.rem(zl + d, 4)
        got(idb.at[other], s_id.at[d - 1])
    for d in (0, 1, 3, 2):
        for r in (0, 1):
            j = lax.rem(zl + d, 4) * 2 + (1 - xs)
            got(q_block(j, r), s_q.at[j, r])

    @pl.when(jnp.logical_not(home))
    def _():
        for d in (0, 1, 3, 2):
            for r in (0, 1):
                j = lax.rem(zl + d, 4) * 2 + xs
                got(q_block(j, r), s_q.at[j, r])

    qrow = span(zl)
    qid = qid_ref[:, qrow].astype(F32)
    lse = lse_ref[:, qrow]

    def match_of(m):
        ids = jnp.broadcast_to(idb[m][0:1, :].astype(F32), (128, BLK)).T
        return ids[:, 0:1] == qid

    def scores(dz, last):
        i = RANK[dz]
        got(a_block(dz, 2, pl.ds(0, ah)), s_ky.at[i, 1])
        got(a_block(dz, 2, pl.ds(ah, ah)), s_ky.at[i, 3])
        if dz == 4:
            got(kb.at[zat(4), pl.ds(a, bh)], s_bz.at[7])
            got(kb.at[zat(4), pl.ds(a + bh, bh)], s_bz.at[8])
        m = lax.rem(zat(dz), 4)
        part = zat(dz) // 4
        for r in (oc, c):
            s = nt(kb[zat(dz)], qb[span(r), span(part, 1024)])
            st[m, r] = st[m, r] + s if last else s
            if last and r is oc:
                send(st.at[m, oc], sx.at[m], s_sx.at[m], partner)

    def probs(dz):
        m = lax.rem(zat(dz), 4)
        got(sx.at[m], s_sx.at[m])
        p = jnp.exp((st[m, c] + sx[m]) * FACTOR - lse)
        st[m, c] = p
        return jnp.sum(jnp.where(match_of(m), p, 0.0), axis=0, keepdims=True)

    for dz in (0, 1, -1, 2):
        scores(dz, False)
    scores(-2, True)
    scores(3, True)
    matched = probs(-2)
    scores(-3, True)
    matched = matched + probs(3)
    scores(4, True)
    matched = matched + probs(-3)
    matched = matched + probs(4)

    mb[0] = jnp.broadcast_to(matched, (8, BLK))
    for d in (1, 3, 2):
        send(mb.at[0], mb.at[4 - d], s_m.at[3 - d], dev(dx=d))
    scale = jnp.float32(GRAD_SCALE) / cnt_ref[:, qrow].astype(F32)
    gap = jnp.exp(gap_ref[:, qrow])
    for d in (1, 3, 2):
        got(mb.at[4 - d], s_m.at[3 - d])
    positive = gap + ((mb[0] + mb[1]) + (mb[2] + mb[3]))[0:1, :]
    inverse = 1.0 / positive

    order = (0, 3, 1, 2)
    for d in order:
        m = lax.rem(zl + d, 4)
        p = st[m, c]
        w = (p - jnp.where(match_of(m), p * inverse, 0.0)) * scale
        wt[m, :, span(c)] = w.astype(BF16)
        blk = wt.at[m, :, span(c)]
        send(blk, blk, s_w.at[m], partner)
        wn[span(c), span(m)] = w.T.astype(BF16)

    def weights_of(d):
        m = lax.rem(zl + d, 4)
        got(wt.at[m, :, span(oc)], s_w.at[m])
        wn[span(oc), span(m)] = wt[m, :, span(oc)].astype(F32).T.astype(BF16)

    def key_part(dz):
        i = RANK[dz]
        m = lax.rem(zat(dz), 4)
        part = zat(dz) // 4
        dkp[i] = (nn(wt[m], qb[:, span(part, 1024)]) * FACTOR).astype(BF16)
        far = span(lax.rem(y + 2, 4))
        for way, rows in ((0, pl.ds(0, ah)), (1, pl.ds(ah, ah))):
            send(dkp.at[i, rows, far], yb.at[i, 2, rows], s_y.at[i, 2 + way], dev(dy=1 + 2 * way))

    def y_pass(*offsets):
        for dz in offsets:
            i = RANK[dz]
            for way, rows in ((0, pl.ds(0, ah)), (1, pl.ds(ah, ah))):
                dy = 1 + 2 * way
                to = span(lax.rem(y + dy, 4))
                got(yb.at[i, 2, rows], s_y.at[i, 2 + way])
                dkp[i, rows, to] = (dkp[i, rows, to].astype(F32) + yb[i, 2, rows].astype(F32)).astype(BF16)
                send(dkp.at[i, pl.ds(0, a), to], yb.at[i, way], s_y.at[i, way], dev(dy=dy))

    def chain(dz, buf, sem, half):
        way = 0 if dz > 0 else 1
        left = abs(dz)
        if left == 3:
            rows = pl.ds(0, half) if dz > 0 else pl.ds(half, half)
        else:
            rows = pl.ds(0, 2 * half)
        got(buf.at[way, left, rows], sem.at[way, left])
        return way, left, rows

    def a_sum(dz):
        i = RANK[dz]
        for s in range(2):
            got(yb.at[i, s], s_y.at[i, s])
        return dkp[i, pl.ds(0, a), ycols].astype(F32) + (yb[i, 0].astype(F32) + yb[i, 1].astype(F32))

    def a_pass(dz):
        i = RANK[dz]
        dkp[i, pl.ds(0, a), ycols] = a_sum(dz).astype(BF16)
        if dz == 4:
            for way, rows in ((0, pl.ds(0, ah)), (1, pl.ds(ah, ah))):
                send(dkp.at[i, rows, ycols], za.at[way, 3, rows], s_za.at[way, 3], dev(dz=1 - 2 * way))
            return
        way, left, rows = chain(dz, za, s_za, ah)
        mine = dkp[i, rows, ycols].astype(F32) + za[way, left, rows].astype(F32)
        dkp[i, rows, ycols] = mine.astype(BF16)
        send(dkp.at[i, pl.ds(0, a), ycols], za.at[way, left - 1], s_za.at[way, left - 1], dev(dz=1 - 2 * way))

    def b_pass(dz):
        i = RANK[dz]
        if dz == 4:
            for way, rows in ((0, 0), (1, bh)):
                src = dkp.at[i, pl.ds(a + rows, bh)]
                send(src, zb.at[way, 3, pl.ds(rows, bh)], s_zb.at[way, 3], dev(dz=1 - 2 * way))
            return
        way, left, rows = chain(dz, zb, s_zb, bh)
        mine = pl.ds(a + rows.start, rows.size)
        dkp[i, mine] = (dkp[i, mine].astype(F32) + zb[way, left, rows].astype(F32)).astype(BF16)
        send(dkp.at[i, pl.ds(a, b)], zb.at[way, left - 1], s_zb.at[way, left - 1], dev(dz=1 - 2 * way))

    def query_part(d, s):
        zf = lax.rem(zl + d, 4)
        j = zf * 2 + s
        keys = kb[pl.ds(pl.multiple_of((zf // 2) * 4, 4), 4), :, span(lax.rem(j, 4))]
        dqp[j] = (nn(wn[...], keys.reshape(1024, BLK)) * FACTOR).astype(BF16)
        to = 2 * s + c
        slot = lax.rem(x - to + 4, 4) - 1
        if s is xs:
            slot = jnp.maximum(slot, 0)
        send(
            dqp.at[j], rb.at[slot, zf], s_r.at[slot, zf], dev(x_to=to),
            when=jnp.logical_not(home) if s is xs else None,
        )

    def query_sum(d):
        zf = lax.rem(zl + d, 4)
        j = zf * 2 + xs

        @pl.when(home)
        def _():
            for s in range(3):
                got(rb.at[s, zf], s_r.at[s, zf])
            total = (dqp[j].astype(F32) + rb[0, zf].astype(F32)) + (
                rb[1, zf].astype(F32) + rb[2, zf].astype(F32)
            )
            dqp[j] = total.astype(BF16)
            if d == 0:
                oq_ref[span(zl), :] = dqp[j, span(c)]

        if d == 0:
            send(dqp.at[j, span(oc)], ab.at[zl], s_a.at[zl], partner, when=home)
        else:
            for r in (0, 1):
                send(dqp.at[j, span(r)], ab.at[zl], s_a.at[zl], dev(zl_to=zf, core=r), when=home)

    far = 1 - xs
    weights_of(0)
    key_part(4)
    b_pass(4)
    weights_of(3)
    key_part(3)
    weights_of(1)
    key_part(-3)
    y_pass(4)
    weights_of(2)
    query_part(2, far)
    query_part(2, xs)
    y_pass(3)
    key_part(2)
    b_pass(3)
    b_pass(-3)
    y_pass(-3)
    key_part(-2)
    query_part(1, far)
    query_part(1, xs)
    a_pass(4)
    key_part(1)
    y_pass(2)
    key_part(-1)
    b_pass(2)
    b_pass(-2)
    y_pass(-2)
    query_part(3, far)
    query_part(3, xs)
    key_part(0)
    y_pass(1)
    a_pass(3)
    a_pass(-3)
    y_pass(-1)
    query_part(0, far)
    query_part(0, xs)
    b_pass(1)
    b_pass(-1)
    y_pass(0)
    query_sum(2)
    a_pass(2)
    a_pass(-2)
    query_sum(1)
    for way in (0, 1):
        got(zb.at[way, 0], s_zb.at[way, 0])
    rest = dkp[0, pl.ds(a, b)].astype(F32) + (zb[0, 0].astype(F32) + zb[1, 0].astype(F32))
    dkp[0, pl.ds(a, b)] = rest.astype(BF16)
    for dy in (1, 3, 2):
        to = span(lax.rem(y + dy, 4))
        send(dkp.at[0, pl.ds(a, b), to], yb2.at[3 - dy], s_y2.at[3 - dy], dev(dy=dy))
    query_sum(3)
    a_pass(1)
    a_pass(-1)
    query_sum(0)
    total = a_sum(0)
    for s in range(3):
        got(yb2.at[s], s_y2.at[s])
    ok_ref[pl.ds(a, b), :] = (dkp[0, pl.ds(a, b), ycols].astype(F32) + yb2[0].astype(F32)) + (
        yb2[1].astype(F32) + yb2[2].astype(F32)
    )
    for d in (2, 1, 3):
        src = lax.rem(zl + d, 4)
        got(ab.at[src], s_a.at[src])
        oq_ref[span(src), :] = ab[src]

    @pl.when(jnp.logical_not(home))
    def _():
        got(ab.at[zl], s_a.at[zl])
        oq_ref[span(zl), :] = ab[zl]

    for way in (0, 1):
        got(za.at[way, 0], s_za.at[way, 0])
    ok_ref[pl.ds(0, a), :] = total + (za[0, 0].astype(F32) + za[1, 0].astype(F32))

    for copy, when in sends:
        if when is None:
            copy.wait_send()
        else:
            pl.when(when)(copy.wait_send)


def on_device(queries, keys, query_ids, memory_ids, target_gap, lse, counts):
    a = ZFIRST
    b = BLK - a
    vmem = pl.BlockSpec(memory_space=pltpu.VMEM)
    dma = pltpu.SemaphoreType.DMA
    query_grad, key_grad = pl.pallas_call(
        kernel,
        out_shape=(
            jax.ShapeDtypeStruct((1024, BLK), BF16),
            jax.ShapeDtypeStruct((BLK, BLK), F32),
        ),
        in_specs=[vmem] * 7,
        out_specs=(vmem, vmem),
        scratch_shapes=[
            pltpu.VMEM((512, 2048), BF16),
            pltpu.VMEM((8, BLK, 1024), BF16),
            pltpu.VMEM((4, 2, BLK, BLK), F32),
            pltpu.VMEM((4, BLK, BLK), F32),
            pltpu.VMEM((4, 8, BLK), jnp.int32),
            pltpu.VMEM((4, 8, BLK), F32),
            pltpu.VMEM((4, BLK, 512), BF16),
            pltpu.VMEM((512, 1024), BF16),
            pltpu.VMEM((8, BLK, 1024), BF16),
            pltpu.VMEM((8, 3, a, BLK), BF16),
            pltpu.VMEM((3, b, BLK), BF16),
            pltpu.VMEM((2, 4, a, BLK), BF16),
            pltpu.VMEM((2, 4, b, 1024), BF16),
            pltpu.VMEM((8, 512, BLK), BF16),
            pltpu.VMEM((3, 4, 512, BLK), BF16),
            pltpu.VMEM((4, BLK, BLK), BF16),
            dma((N_SENDS,)),
            dma((9,)),
            dma((8, 4)),
            dma((9,)),
            dma((3,)),
            dma((8, 2)),
            dma((3,)),
            dma((4,)),
            dma((3,)),
            dma((4,)),
            dma((8, 4)),
            dma((3,)),
            dma((2, 4)),
            dma((2, 4)),
            dma((3, 4)),
            dma((4,)),
        ],
        compiler_params=pltpu.CompilerParams(
            collective_id=0, has_side_effects=True, vmem_limit_bytes=56 * 2**20
        ),
        cost_estimate=pl.CostEstimate(
            flops=6_442_450_944, bytes_accessed=3_000_000, transcendentals=262_144
        ),
        name="contrastive_backward",
    )(
        queries,
        keys,
        query_ids.reshape(1, -1),
        memory_ids.reshape(1, -1),
        target_gap.reshape(1, -1),
        lse.reshape(1, -1),
        counts.reshape(1, -1),
    )
    return query_grad.astype(F32), key_grad


def solution(mesh):
    torus = Mesh(mesh.devices.reshape(2, 4, 2, 4, 4), AXES)
    return jax.shard_map(
        on_device,
        mesh=torus,
        in_specs=(P(PB, MA), P(MA, PB), P(PB), P(MA), P(PB), P(PB), P(PB)),
        out_specs=(P(PB, MA), P(MA, PB)),
        check_vma=False,
    )
```

```python
import math

import jax
import jax.numpy as jnp
from jax import lax
from jax.experimental import pallas as pl
from jax.experimental.pallas import tpu as pltpu
from jax.sharding import Mesh
from jax.sharding import PartitionSpec as P

D = 4096
GRAD_SCALE = 1024
AXES = ("zh", "y", "core", "zl", "x")
PB = ("zh", "y", "core")
MA = ("zl", "x")
FACTOR = 1.0 / math.sqrt(D)
BLK = 256
ZFIRST = 192
F32 = jnp.float32
BF16 = jnp.bfloat16
OFFSETS = (0, 1, -1, 2, -2, 3, -3, 4)
RANK = {dz: i for i, dz in enumerate(OFFSETS)}
N_SENDS = 200


def nt(a, b):
    return lax.dot_general(a, b, (((1,), (1,)), ((), ())), preferred_element_type=F32)


def nn(a, b):
    return jnp.dot(a, b, preferred_element_type=F32)


def kernel(
    q_ref, k_ref, qid_ref, mid_ref, gap_ref, lse_ref, cnt_ref, oq_ref, ok_ref,
    qb, kb, st, sx, idb, mb, wt, wn, dkp, yb, yb2, za, zb, dqp, rb, ab,
    ssem, s_kz, s_ky, s_bz, s_by, s_q, s_id, s_sx, s_m, s_w, s_y, s_y2, s_za, s_zb, s_r, s_a,
):
    zh, y, c, zl, x = [lax.axis_index(a) for a in AXES]
    z = zh * 4 + zl
    xp = lax.rem(x, 2)
    xs = x // 2
    home = xp == c
    oc = 1 - c
    a = ZFIRST
    ah = a // 2
    b = BLK - a
    bh = b // 2

    def zat(dz):
        return lax.rem(z + dz + 8, 8)

    def dev(dx=0, dy=0, dz=0, core=None, zl_to=None, x_to=None):
        zz = zat(dz)
        return (
            zz // 4,
            lax.rem(y + dy, 4),
            c if core is None else core,
            lax.rem(zz, 4) if zl_to is None else zl_to,
            lax.rem(x + dx, 4) if x_to is None else x_to,
        )

    def span(i, n=BLK):
        return pl.ds(pl.multiple_of(i * n, n), n)

    sends = []

    def send(src, dst, recv, to, when=None):
        copy = pltpu.make_async_remote_copy(
            src_ref=src,
            dst_ref=dst,
            send_sem=ssem.at[len(sends)],
            recv_sem=recv,
            device_id=to,
            device_id_type=pl.DeviceIdType.MESH,
        )
        if when is None:
            copy.start()
        else:
            pl.when(when)(copy.start)
        sends.append((copy, when))

    partner = dev(core=oc)

    def got(dst, recv):
        pltpu.make_async_remote_copy(
            src_ref=dst,
            dst_ref=dst,
            send_sem=ssem.at[0],
            recv_sem=recv,
            device_id=partner,
            device_id_type=pl.DeviceIdType.MESH,
        ).wait_recv()

    barrier = pltpu.get_barrier_semaphore()
    peers = [partner, dev(dz=1), dev(dz=-1)]
    for d in (1, 2, 3):
        other = lax.rem(zl + d, 4)
        peers += [dev(dx=d), dev(dy=d), dev(zl_to=other), dev(zl_to=other, core=oc)]
    for peer in peers:
        pl.semaphore_signal(barrier, inc=1, device_id=peer, device_id_type=pl.DeviceIdType.MESH)
    ycols = span(y)
    kb[z, :, ycols] = k_ref[...]
    idb[zl] = jnp.broadcast_to(mid_ref[...], (8, BLK))
    pl.semaphore_wait(barrier, len(peers))

    def zslot(dz):
        return kb.at[zat(dz)]

    def a_block(dz, dy, rows):
        return kb.at[zat(dz), rows, span(lax.rem(y + dy, 4))]

    def a_z(dz, step, rows, part):
        blk = a_block(dz, 0, rows)
        to = dz - step
        i = 8 if part == 1 else RANK[4 if to == -4 else to]
        send(blk, blk, s_kz.at[i], dev(dz=step))

    def a_y(dz):
        blk = a_block(dz, 0, pl.ds(0, a))
        for dy in (1, 3):
            send(blk, blk, s_ky.at[RANK[dz], 3 - dy], dev(dy=dy))

    def a_relay(*offsets):
        for dz in offsets:
            i = RANK[dz]
            got(a_block(dz, 3, pl.ds(0, a)), s_ky.at[i, 2])
            blk = a_block(dz, 3, pl.ds(0, ah))
            send(blk, blk, s_ky.at[i, 1], dev(dy=1))
            got(a_block(dz, 1, pl.ds(0, a)), s_ky.at[i, 0])
            blk = a_block(dz, 1, pl.ds(ah, ah))
            send(blk, blk, s_ky.at[i, 3], dev(dy=3))

    def a_arrive(dz):
        for sign in (-1, 1) if dz < 4 else (0,):
            if dz == 4:
                got(a_block(4, 0, pl.ds(0, ah)), s_kz.at[7])
                got(a_block(4, 0, pl.ds(ah, ah)), s_kz.at[8])
                a_y(4)
                continue
            at = sign * dz
            got(a_block(at, 0, pl.ds(0, a)), s_kz.at[RANK[at]])
            if dz < 3:
                a_z(at, -sign, pl.ds(0, a), 0)
            elif sign < 0:
                a_z(at, 1, pl.ds(0, ah), 0)
            else:
                a_z(at, -1, pl.ds(ah, ah), 1)
        if dz < 4:
            a_y(-dz)
            a_y(dz)

    def b_z(dz, step, rows, part):
        blk = kb.at[zat(dz), rows]
        to = dz - step
        i = 8 if part == 1 else RANK[4 if to == -4 else to]
        send(blk, blk, s_bz.at[i], dev(dz=step))

    def b_arrive(dz):
        for sign in (-1, 1):
            at = sign * dz
            got(kb.at[zat(at), pl.ds(a, b)], s_bz.at[RANK[at]])
            if dz < 3:
                b_z(at, -sign, pl.ds(a, b), 0)
            elif sign < 0:
                b_z(at, 1, pl.ds(a, bh), 0)
            else:
                b_z(at, -1, pl.ds(a + bh, bh), 1)

    def q_block(j, r):
        return qb.at[span(r), span(j)]

    def zl_of(d):
        return (zl, zl + 1 - 2 * lax.rem(zl, 2), lax.rem(zl + 2, 4), 3 - zl)[d]

    j_own = zl * 2 + xs
    for d in (1, 2, 3):
        send(idb.at[zl], idb.at[zl], s_id.at[3 - d], dev(zl_to=lax.rem(zl + d, 4)))
    send(q_ref.at[span(zl)], q_block(j_own, c), s_q.at[j_own, c], dev(core=xp), when=jnp.logical_not(home))
    a_z(0, 1, pl.ds(0, a), 0)
    a_z(0, -1, pl.ds(0, a), 0)
    for d in (1, 2, 3):
        to = zl_of(d)
        send(q_ref.at[span(to)], q_block(j_own, c), s_q.at[j_own, c], dev(zl_to=to, core=xp))
    blk = a_block(0, 0, pl.ds(a, b))
    for dy in (1, 3, 2):
        send(blk, blk, s_by.at[3 - dy], dev(dy=dy))
    a_y(0)

    @pl.when(home)
    def _():
        qb[span(c), span(j_own)] = q_ref[span(zl), :]

    def q_spread(j, r, wait):
        if wait:
            pl.when(home)(lambda: got(q_block(j, r), s_q.at[j, r]))
        for dx in (1, 3):
            send(q_block(j, r), q_block(j, r), s_q.at[j, r], dev(dx=dx), when=home)

    def q_arrive(d):
        j = zl_of(d) * 2 + xs
        q_spread(j, 0, True)
        q_spread(j, 1, True)

    away = jnp.logical_not(home)

    def q_from(dx, d):
        return zl_of(d) * 2 + lax.rem(x + dx, 4) // 2

    def q_relay(d):
        for r, dx in ((0, 3), (1, 1)):
            blk = q_block(q_from(dx, d), r)
            sem = s_q.at[q_from(dx, d), r]
            pl.when(away)(lambda: got(blk, sem))
            send(blk, blk, sem, dev(dx=4 - dx), when=away)

    q_spread(j_own, c, False)
    q_spread(j_own, oc, True)
    a_arrive(1)
    a_relay(0)
    for dy in (1, 3, 2):
        got(a_block(0, 4 - dy, pl.ds(a, b)), s_by.at[3 - dy])
    b_z(0, 1, pl.ds(a, b), 0)
    b_z(0, -1, pl.ds(a, b), 0)
    q_arrive(1)
    q_relay(0)
    a_arrive(2)
    a_relay(1)
    q_arrive(2)
    b_arrive(1)
    q_relay(1)
    a_arrive(3)
    a_relay(-1)
    q_arrive(3)
    b_arrive(2)
    q_relay(2)
    a_arrive(4)
    a_relay(2)
    b_arrive(3)
    q_relay(3)
    a_relay(-2)
    a_relay(3)
    a_relay(-3)
    a_relay(4)

    for d in (1, 3, 2):
        other = lax.rem(zl + d, 4)
        got(idb.at[other], s_id.at[d - 1])

    @pl.when(home)
    def _():
        for d in (0, 1, 2, 3):
            for r in (0, 1):
                j = zl_of(d) * 2 + (1 - xs)
                got(q_block(j, r), s_q.at[j, r])

    @pl.when(away)
    def _():
        for d in (0, 1, 2, 3):
            for r, dx in ((1, 3), (0, 1)):
                j = q_from(dx, d)
                got(q_block(j, r), s_q.at[j, r])

    qrow = span(zl)
    qid = qid_ref[:, qrow].astype(F32)
    lse = lse_ref[:, qrow]

    def match_of(m):
        ids = jnp.broadcast_to(idb[m][0:1, :].astype(F32), (128, BLK)).T
        return ids[:, 0:1] == qid

    def scores(dz, last):
        i = RANK[dz]
        got(a_block(dz, 2, pl.ds(0, ah)), s_ky.at[i, 1])
        got(a_block(dz, 2, pl.ds(ah, ah)), s_ky.at[i, 3])
        if dz == 4:
            got(kb.at[zat(4), pl.ds(a, bh)], s_bz.at[7])
            got(kb.at[zat(4), pl.ds(a + bh, bh)], s_bz.at[8])
        m = lax.rem(zat(dz), 4)
        part = zat(dz) // 4
        for r in (oc, c):
            s = nt(kb[zat(dz)], qb[span(r), span(part, 1024)])
            st[m, r] = st[m, r] + s if last else s
            if last and r is oc:
                send(st.at[m, oc], sx.at[m], s_sx.at[m], partner)

    def probs(dz):
        m = lax.rem(zat(dz), 4)
        got(sx.at[m], s_sx.at[m])
        p = jnp.exp((st[m, c] + sx[m]) * FACTOR - lse)
        st[m, c] = p
        return jnp.sum(jnp.where(match_of(m), p, 0.0), axis=0, keepdims=True)

    for dz in (0, 1, -1, 2):
        scores(dz, False)
    scores(-2, True)
    scores(3, True)
    matched = probs(-2)
    scores(-3, True)
    matched = matched + probs(3)
    scores(4, True)
    matched = matched + probs(-3)
    matched = matched + probs(4)

    mb[0] = jnp.broadcast_to(matched, (8, BLK))
    for d in (1, 3, 2):
        send(mb.at[0], mb.at[4 - d], s_m.at[3 - d], dev(dx=d))
    scale = jnp.float32(GRAD_SCALE) / cnt_ref[:, qrow].astype(F32)
    gap = jnp.exp(gap_ref[:, qrow])
    for d in (1, 3, 2):
        got(mb.at[4 - d], s_m.at[3 - d])
    positive = gap + ((mb[0] + mb[1]) + (mb[2] + mb[3]))[0:1, :]
    inverse = 1.0 / positive

    order = (0, 3, 1, 2)
    for d in order:
        m = lax.rem(zl + d, 4)
        p = st[m, c]
        w = (p - jnp.where(match_of(m), p * inverse, 0.0)) * scale
        wt[m, :, span(c)] = w.astype(BF16)
        blk = wt.at[m, :, span(c)]
        send(blk, blk, s_w.at[m], partner)
        wn[span(c), span(m)] = w.T.astype(BF16)

    def weights_of(d):
        m = lax.rem(zl + d, 4)
        got(wt.at[m, :, span(oc)], s_w.at[m])
        wn[span(oc), span(m)] = wt[m, :, span(oc)].astype(F32).T.astype(BF16)

    def key_part(dz):
        i = RANK[dz]
        m = lax.rem(zat(dz), 4)
        part = zat(dz) // 4
        dkp[i] = (nn(wt[m], qb[:, span(part, 1024)]) * FACTOR).astype(BF16)
        far = span(lax.rem(y + 2, 4))
        for way, rows in ((0, pl.ds(0, ah)), (1, pl.ds(ah, ah))):
            send(dkp.at[i, rows, far], yb.at[i, 2, rows], s_y.at[i, 2 + way], dev(dy=1 + 2 * way))

    def y_pass(*offsets):
        for dz in offsets:
            i = RANK[dz]
            for way, rows in ((0, pl.ds(0, ah)), (1, pl.ds(ah, ah))):
                dy = 1 + 2 * way
                to = span(lax.rem(y + dy, 4))
                got(yb.at[i, 2, rows], s_y.at[i, 2 + way])
                dkp[i, rows, to] = (dkp[i, rows, to].astype(F32) + yb[i, 2, rows].astype(F32)).astype(BF16)
                send(dkp.at[i, pl.ds(0, a), to], yb.at[i, way], s_y.at[i, way], dev(dy=dy))

    def chain(dz, buf, sem, half):
        way = 0 if dz > 0 else 1
        left = abs(dz)
        if left == 3:
            rows = pl.ds(0, half) if dz > 0 else pl.ds(half, half)
        else:
            rows = pl.ds(0, 2 * half)
        got(buf.at[way, left, rows], sem.at[way, left])
        return way, left, rows

    def a_sum(dz):
        i = RANK[dz]
        for s in range(2):
            got(yb.at[i, s], s_y.at[i, s])
        return dkp[i, pl.ds(0, a), ycols].astype(F32) + (yb[i, 0].astype(F32) + yb[i, 1].astype(F32))

    def a_pass(dz):
        i = RANK[dz]
        dkp[i, pl.ds(0, a), ycols] = a_sum(dz).astype(BF16)
        if dz == 4:
            for way, rows in ((0, pl.ds(0, ah)), (1, pl.ds(ah, ah))):
                send(dkp.at[i, rows, ycols], za.at[way, 3, rows], s_za.at[way, 3], dev(dz=1 - 2 * way))
            return
        way, left, rows = chain(dz, za, s_za, ah)
        mine = dkp[i, rows, ycols].astype(F32) + za[way, left, rows].astype(F32)
        dkp[i, rows, ycols] = mine.astype(BF16)
        send(dkp.at[i, pl.ds(0, a), ycols], za.at[way, left - 1], s_za.at[way, left - 1], dev(dz=1 - 2 * way))

    def b_pass(dz):
        i = RANK[dz]
        if dz == 4:
            for way, rows in ((0, 0), (1, bh)):
                src = dkp.at[i, pl.ds(a + rows, bh)]
                send(src, zb.at[way, 3, pl.ds(rows, bh)], s_zb.at[way, 3], dev(dz=1 - 2 * way))
            return
        way, left, rows = chain(dz, zb, s_zb, bh)
        mine = pl.ds(a + rows.start, rows.size)
        dkp[i, mine] = (dkp[i, mine].astype(F32) + zb[way, left, rows].astype(F32)).astype(BF16)
        send(dkp.at[i, pl.ds(a, b)], zb.at[way, left - 1], s_zb.at[way, left - 1], dev(dz=1 - 2 * way))

    def query_part(d, s):
        zf = lax.rem(zl + d, 4)
        j = zf * 2 + s
        keys = kb[pl.ds(pl.multiple_of((zf // 2) * 4, 4), 4), :, span(lax.rem(j, 4))]
        dqp[j] = (nn(wn[...], keys.reshape(1024, BLK)) * FACTOR).astype(BF16)
        to = 2 * s + c
        slot = lax.rem(x - to + 4, 4) - 1
        if s is xs:
            slot = jnp.maximum(slot, 0)
        send(
            dqp.at[j], rb.at[slot, zf], s_r.at[slot, zf], dev(x_to=to),
            when=jnp.logical_not(home) if s is xs else None,
        )

    def query_sum(d):
        zf = lax.rem(zl + d, 4)
        j = zf * 2 + xs

        @pl.when(home)
        def _():
            for s in range(3):
                got(rb.at[s, zf], s_r.at[s, zf])
            total = (dqp[j].astype(F32) + rb[0, zf].astype(F32)) + (
                rb[1, zf].astype(F32) + rb[2, zf].astype(F32)
            )
            dqp[j] = total.astype(BF16)
            if d == 0:
                oq_ref[span(zl), :] = dqp[j, span(c)]

        if d == 0:
            send(dqp.at[j, span(oc)], ab.at[zl], s_a.at[zl], partner, when=home)
        else:
            for r in (0, 1):
                send(dqp.at[j, span(r)], ab.at[zl], s_a.at[zl], dev(zl_to=zf, core=r), when=home)

    far = 1 - xs
    weights_of(0)
    key_part(4)
    b_pass(4)
    weights_of(3)
    key_part(3)
    weights_of(1)
    key_part(-3)
    weights_of(2)
    query_part(2, far)
    query_part(2, xs)
    y_pass(4)
    key_part(2)
    query_part(1, far)
    query_part(1, xs)
    b_pass(3)
    b_pass(-3)
    y_pass(3)
    key_part(-2)
    query_part(3, far)
    query_part(3, xs)
    y_pass(-3)
    key_part(1)
    query_part(0, far)
    query_part(0, xs)
    key_part(-1)
    a_pass(4)
    y_pass(2)
    key_part(0)
    b_pass(2)
    b_pass(-2)
    y_pass(-2)
    a_pass(3)
    a_pass(-3)
    y_pass(1)
    b_pass(1)
    b_pass(-1)
    y_pass(-1)
    query_sum(2)
    a_pass(2)
    a_pass(-2)
    y_pass(0)
    query_sum(1)
    for way in (0, 1):
        got(zb.at[way, 0], s_zb.at[way, 0])
    rest = dkp[0, pl.ds(a, b)].astype(F32) + (zb[0, 0].astype(F32) + zb[1, 0].astype(F32))
    dkp[0, pl.ds(a, b)] = rest.astype(BF16)
    for dy in (1, 3, 2):
        to = span(lax.rem(y + dy, 4))
        send(dkp.at[0, pl.ds(a, b), to], yb2.at[3 - dy], s_y2.at[3 - dy], dev(dy=dy))
    query_sum(3)
    a_pass(1)
    a_pass(-1)
    query_sum(0)
    total = a_sum(0)
    for s in range(3):
        got(yb2.at[s], s_y2.at[s])
    ok_ref[pl.ds(a, b), :] = (dkp[0, pl.ds(a, b), ycols].astype(F32) + yb2[0].astype(F32)) + (
        yb2[1].astype(F32) + yb2[2].astype(F32)
    )
    for d in (2, 1, 3):
        src = lax.rem(zl + d, 4)
        got(ab.at[src], s_a.at[src])
        oq_ref[span(src), :] = ab[src]

    @pl.when(jnp.logical_not(home))
    def _():
        got(ab.at[zl], s_a.at[zl])
        oq_ref[span(zl), :] = ab[zl]

    for way in (0, 1):
        got(za.at[way, 0], s_za.at[way, 0])
    ok_ref[pl.ds(0, a), :] = total + (za[0, 0].astype(F32) + za[1, 0].astype(F32))

    for copy, when in sends:
        if when is None:
            copy.wait_send()
        else:
            pl.when(when)(copy.wait_send)


def on_device(queries, keys, query_ids, memory_ids, target_gap, lse, counts):
    a = ZFIRST
    b = BLK - a
    vmem = pl.BlockSpec(memory_space=pltpu.VMEM)
    dma = pltpu.SemaphoreType.DMA
    query_grad, key_grad = pl.pallas_call(
        kernel,
        out_shape=(
            jax.ShapeDtypeStruct((1024, BLK), BF16),
            jax.ShapeDtypeStruct((BLK, BLK), F32),
        ),
        in_specs=[vmem] * 7,
        out_specs=(vmem, vmem),
        scratch_shapes=[
            pltpu.VMEM((512, 2048), BF16),
            pltpu.VMEM((8, BLK, 1024), BF16),
            pltpu.VMEM((4, 2, BLK, BLK), F32),
            pltpu.VMEM((4, BLK, BLK), F32),
            pltpu.VMEM((4, 8, BLK), jnp.int32),
            pltpu.VMEM((4, 8, BLK), F32),
            pltpu.VMEM((4, BLK, 512), BF16),
            pltpu.VMEM((512, 1024), BF16),
            pltpu.VMEM((8, BLK, 1024), BF16),
            pltpu.VMEM((8, 3, a, BLK), BF16),
            pltpu.VMEM((3, b, BLK), BF16),
            pltpu.VMEM((2, 4, a, BLK), BF16),
            pltpu.VMEM((2, 4, b, 1024), BF16),
            pltpu.VMEM((8, 512, BLK), BF16),
            pltpu.VMEM((3, 4, 512, BLK), BF16),
            pltpu.VMEM((4, BLK, BLK), BF16),
            dma((N_SENDS,)),
            dma((9,)),
            dma((8, 4)),
            dma((9,)),
            dma((3,)),
            dma((8, 2)),
            dma((3,)),
            dma((4,)),
            dma((3,)),
            dma((4,)),
            dma((8, 4)),
            dma((3,)),
            dma((2, 4)),
            dma((2, 4)),
            dma((3, 4)),
            dma((4,)),
        ],
        compiler_params=pltpu.CompilerParams(
            collective_id=0, has_side_effects=True, vmem_limit_bytes=56 * 2**20
        ),
        cost_estimate=pl.CostEstimate(
            flops=6_442_450_944, bytes_accessed=3_000_000, transcendentals=262_144
        ),
        name="contrastive_backward",
    )(
        queries,
        keys,
        query_ids.reshape(1, -1),
        memory_ids.reshape(1, -1),
        target_gap.reshape(1, -1),
        lse.reshape(1, -1),
        counts.reshape(1, -1),
    )
    return query_grad.astype(F32), key_grad


def solution(mesh):
    torus = Mesh(mesh.devices.reshape(2, 4, 2, 4, 4), AXES)
    return jax.shard_map(
        on_device,
        mesh=torus,
        in_specs=(P(PB, MA), P(MA, PB), P(PB), P(MA), P(PB), P(PB), P(PB)),
        out_specs=(P(PB, MA), P(MA, PB)),
        check_vma=False,
    )
```

```python
import math

import jax
import jax.numpy as jnp
from jax import lax
from jax.experimental import pallas as pl
from jax.experimental.pallas import tpu as pltpu
from jax.sharding import Mesh
from jax.sharding import PartitionSpec as P

D = 4096
GRAD_SCALE = 1024
AXES = ("zh", "y", "core", "zl", "x")
PB = ("zh", "y", "core")
MA = ("zl", "x")
FACTOR = 1.0 / math.sqrt(D)
BLK = 256
ZFIRST = 192
F32 = jnp.float32
BF16 = jnp.bfloat16
OFFSETS = (0, 1, -1, 2, -2, 3, -3, 4)
RANK = {dz: i for i, dz in enumerate(OFFSETS)}
N_SENDS = 200


def nt(a, b):
    return lax.dot_general(a, b, (((1,), (1,)), ((), ())), preferred_element_type=F32)


def nn(a, b):
    return jnp.dot(a, b, preferred_element_type=F32)


def kernel(
    q_ref, k_ref, qid_ref, mid_ref, gap_ref, lse_ref, cnt_ref, oq_ref, ok_ref,
    qb, kb, st, sx, idb, mb, wt, wn, dkp, yb, yb2, za, zb, dqp, rb,
    ssem, s_own, s_kz, s_ky, s_bz, s_by, s_q, s_id, s_sx, s_m, s_w, s_y, s_y2, s_za, s_zb, s_r, s_a,
):
    zh, y, c, zl, x = [lax.axis_index(a) for a in AXES]
    z = zh * 4 + zl
    xp = lax.rem(x, 2)
    xs = x // 2
    home = xp == c
    oc = 1 - c
    a = ZFIRST
    ah = a // 2
    b = BLK - a
    bh = b // 2

    def zat(dz):
        return lax.rem(z + dz + 8, 8)

    def dev(dx=0, dy=0, dz=0, core=None, zl_to=None, x_to=None):
        zz = zat(dz)
        return (
            zz // 4,
            lax.rem(y + dy, 4),
            c if core is None else core,
            lax.rem(zz, 4) if zl_to is None else zl_to,
            lax.rem(x + dx, 4) if x_to is None else x_to,
        )

    def span(i, n=BLK):
        return pl.ds(pl.multiple_of(i * n, n), n)

    sends = []

    def send(src, dst, recv, to, when=None):
        copy = pltpu.make_async_remote_copy(
            src_ref=src,
            dst_ref=dst,
            send_sem=ssem.at[len(sends)],
            recv_sem=recv,
            device_id=to,
            device_id_type=pl.DeviceIdType.MESH,
        )
        if when is None:
            copy.start()
        else:
            pl.when(when)(copy.start)
        sends.append((copy, when))

    partner = dev(core=oc)

    def got(dst, recv):
        pltpu.make_async_remote_copy(
            src_ref=dst,
            dst_ref=dst,
            send_sem=ssem.at[0],
            recv_sem=recv,
            device_id=partner,
            device_id_type=pl.DeviceIdType.MESH,
        ).wait_recv()

    barrier = pltpu.get_barrier_semaphore()
    peers = [partner, dev(dz=1), dev(dz=-1)]
    for d in (1, 2, 3):
        other = lax.rem(zl + d, 4)
        peers += [dev(dx=d), dev(dy=d), dev(zl_to=other), dev(zl_to=other, core=oc)]
    for peer in peers:
        pl.semaphore_signal(barrier, inc=1, device_id=peer, device_id_type=pl.DeviceIdType.MESH)
    ycols = span(y)
    own_keys = pltpu.make_async_copy(k_ref, kb.at[z, :, ycols], s_own.at[0])
    own_keys.start()
    idb[zl] = jnp.broadcast_to(mid_ref[...], (8, BLK))
    pl.semaphore_wait(barrier, len(peers))

    def zslot(dz):
        return kb.at[zat(dz)]

    def a_block(dz, dy, rows):
        return kb.at[zat(dz), rows, span(lax.rem(y + dy, 4))]

    def a_z(dz, step, rows, part):
        blk = a_block(dz, 0, rows)
        to = dz - step
        i = 8 if part == 1 else RANK[4 if to == -4 else to]
        send(k_ref.at[rows] if dz == 0 else blk, blk, s_kz.at[i], dev(dz=step))

    def a_y(dz):
        blk = a_block(dz, 0, pl.ds(0, a))
        for dy in (1, 3):
            send(k_ref.at[pl.ds(0, a)] if dz == 0 else blk, blk, s_ky.at[RANK[dz], 3 - dy], dev(dy=dy))

    def a_relay(*offsets):
        for dz in offsets:
            i = RANK[dz]
            got(a_block(dz, 3, pl.ds(0, a)), s_ky.at[i, 2])
            blk = a_block(dz, 3, pl.ds(0, ah))
            send(blk, blk, s_ky.at[i, 1], dev(dy=1))
            got(a_block(dz, 1, pl.ds(0, a)), s_ky.at[i, 0])
            blk = a_block(dz, 1, pl.ds(ah, ah))
            send(blk, blk, s_ky.at[i, 3], dev(dy=3))

    def a_arrive(dz):
        for sign in (-1, 1) if dz < 4 else (0,):
            if dz == 4:
                got(a_block(4, 0, pl.ds(0, ah)), s_kz.at[7])
                got(a_block(4, 0, pl.ds(ah, ah)), s_kz.at[8])
                a_y(4)
                continue
            at = sign * dz
            got(a_block(at, 0, pl.ds(0, a)), s_kz.at[RANK[at]])
            if dz < 3:
                a_z(at, -sign, pl.ds(0, a), 0)
            elif sign < 0:
                a_z(at, 1, pl.ds(0, ah), 0)
            else:
                a_z(at, -1, pl.ds(ah, ah), 1)
        if dz < 4:
            a_y(-dz)
            a_y(dz)

    def b_z(dz, step, rows, part):
        blk = kb.at[zat(dz), rows]
        to = dz - step
        i = 8 if part == 1 else RANK[4 if to == -4 else to]
        send(blk, blk, s_bz.at[i], dev(dz=step))

    def b_arrive(dz):
        for sign in (-1, 1):
            at = sign * dz
            got(kb.at[zat(at), pl.ds(a, b)], s_bz.at[RANK[at]])
            if dz < 3:
                b_z(at, -sign, pl.ds(a, b), 0)
            elif sign < 0:
                b_z(at, 1, pl.ds(a, bh), 0)
            else:
                b_z(at, -1, pl.ds(a + bh, bh), 1)

    def q_block(j, r):
        return qb.at[span(r), span(j)]

    def zl_of(d):
        return (zl, zl + 1 - 2 * lax.rem(zl, 2), lax.rem(zl + 2, 4), 3 - zl)[d]

    j_own = zl * 2 + xs
    for d in (1, 2, 3):
        send(idb.at[zl], idb.at[zl], s_id.at[3 - d], dev(zl_to=lax.rem(zl + d, 4)))
    send(q_ref.at[span(zl)], q_block(j_own, c), s_q.at[j_own, c], dev(core=xp), when=jnp.logical_not(home))
    a_z(0, 1, pl.ds(0, a), 0)
    a_z(0, -1, pl.ds(0, a), 0)

    def q_exchange(d):
        to = zl_of(d)
        send(q_ref.at[span(to)], q_block(j_own, c), s_q.at[j_own, c], dev(zl_to=to, core=xp))
    blk = a_block(0, 0, pl.ds(a, b))
    for dy in (1, 3, 2):
        send(k_ref.at[pl.ds(a, b)], blk, s_by.at[3 - dy], dev(dy=dy))
    a_y(0)

    own_queries = pltpu.make_async_copy(q_ref.at[span(zl)], q_block(j_own, c), s_own.at[1])
    pl.when(home)(own_queries.start)

    def q_spread(j, r, own=False):
        if not own:
            pl.when(home)(lambda: got(q_block(j, r), s_q.at[j, r]))
        src = q_ref.at[span(zl)] if own else q_block(j, r)
        for dx in (1, 3):
            send(src, q_block(j, r), s_q.at[j, r], dev(dx=dx), when=home)

    def q_arrive(d):
        j = zl_of(d) * 2 + xs
        q_spread(j, 0)
        q_spread(j, 1)

    away = jnp.logical_not(home)

    def q_from(dx, d):
        return zl_of(d) * 2 + lax.rem(x + dx, 4) // 2

    def q_relay(d):
        for r, dx in ((0, 3), (1, 1)):
            blk = q_block(q_from(dx, d), r)
            sem = s_q.at[q_from(dx, d), r]
            pl.when(away)(lambda: got(blk, sem))
            send(blk, blk, sem, dev(dx=4 - dx), when=away)

    qrow = span(zl)
    qid = qid_ref[:, qrow].astype(F32)
    lse = lse_ref[:, qrow]

    def match_of(m):
        ids = jnp.broadcast_to(idb[m][0:1, :].astype(F32), (128, BLK)).T
        return ids[:, 0:1] == qid

    def scores(dz, last):
        i = RANK[dz]
        got(a_block(dz, 2, pl.ds(0, ah)), s_ky.at[i, 1])
        got(a_block(dz, 2, pl.ds(ah, ah)), s_ky.at[i, 3])
        if dz == 4:
            got(kb.at[zat(4), pl.ds(a, bh)], s_bz.at[7])
            got(kb.at[zat(4), pl.ds(a + bh, bh)], s_bz.at[8])
        m = lax.rem(zat(dz), 4)
        part = zat(dz) // 4
        for r in (oc, c):
            s = nt(kb[zat(dz)], qb[span(r), span(part, 1024)])
            st[m, r] = st[m, r] + s if last else s
            if last and r is oc:
                send(st.at[m, oc], sx.at[m], s_sx.at[m], partner)

    def probs(dz):
        m = lax.rem(zat(dz), 4)
        got(sx.at[m], s_sx.at[m])
        p = jnp.exp((st[m, c] + sx[m]) * FACTOR - lse)
        st[m, c] = p
        return jnp.sum(jnp.where(match_of(m), p, 0.0), axis=0, keepdims=True)

    q_exchange(3)
    q_spread(j_own, c, own=True)
    q_spread(j_own, oc)
    pl.when(home)(own_queries.wait)
    a_arrive(1)
    q_exchange(1)
    q_exchange(2)
    a_relay(0)
    a_relay(1)
    own_keys.wait()
    for dy in (1, 3, 2):
        got(a_block(0, 4 - dy, pl.ds(a, b)), s_by.at[3 - dy])
    b_z(0, 1, pl.ds(a, b), 0)
    b_z(0, -1, pl.ds(a, b), 0)
    q_relay(0)
    q_arrive(3)
    q_arrive(1)
    a_arrive(2)
    q_arrive(2)
    b_arrive(1)
    q_relay(1)
    a_relay(-1)
    a_arrive(3)
    b_arrive(2)
    a_arrive(4)
    a_relay(2)
    q_relay(3)
    q_relay(2)
    b_arrive(3)
    a_relay(-2)
    a_relay(3)
    a_relay(-3)
    for d in (1, 3, 2):
        other = lax.rem(zl + d, 4)
        got(idb.at[other], s_id.at[d - 1])

    @pl.when(home)
    def _():
        for d in (0, 1, 2, 3):
            for r in (0, 1):
                j = zl_of(d) * 2 + (1 - xs)
                got(q_block(j, r), s_q.at[j, r])

    @pl.when(away)
    def _():
        for d in (0, 1, 2, 3):
            for r, dx in ((1, 3), (0, 1)):
                j = q_from(dx, d)
                got(q_block(j, r), s_q.at[j, r])

    scores(0, False)
    scores(1, False)
    a_relay(4)
    scores(-1, False)
    scores(2, False)
    scores(-2, True)
    scores(3, True)
    matched = probs(-2)
    scores(-3, True)
    matched = matched + probs(3)
    scores(4, True)
    matched = matched + probs(-3)
    matched = matched + probs(4)

    mb[0] = jnp.broadcast_to(matched, (8, BLK))
    for d in (1, 3, 2):
        send(mb.at[0], mb.at[4 - d], s_m.at[3 - d], dev(dx=d))
    scale = jnp.float32(GRAD_SCALE) / cnt_ref[:, qrow].astype(F32)
    gap = jnp.exp(gap_ref[:, qrow])
    for d in (1, 3, 2):
        got(mb.at[4 - d], s_m.at[3 - d])
    positive = gap + ((mb[0] + mb[1]) + (mb[2] + mb[3]))[0:1, :]
    inverse = 1.0 / positive

    order = (0, 3, 1, 2)
    for d in order:
        m = lax.rem(zl + d, 4)
        p = st[m, c]
        w = (p - jnp.where(match_of(m), p * inverse, 0.0)) * scale
        wt[m, :, span(c)] = w.astype(BF16)
        blk = wt.at[m, :, span(c)]
        send(blk, blk, s_w.at[m], partner)
        wn[span(c), span(m)] = w.T.astype(BF16)

    def weights_of(d):
        m = lax.rem(zl + d, 4)
        got(wt.at[m, :, span(oc)], s_w.at[m])
        wn[span(oc), span(m)] = wt[m, :, span(oc)].astype(F32).T.astype(BF16)

    def key_part(dz):
        i = RANK[dz]
        m = lax.rem(zat(dz), 4)
        part = zat(dz) // 4
        dkp[i] = (nn(wt[m], qb[:, span(part, 1024)]) * FACTOR).astype(BF16)
        far = span(lax.rem(y + 2, 4))
        for way, rows in ((0, pl.ds(0, ah)), (1, pl.ds(ah, ah))):
            send(dkp.at[i, rows, far], yb.at[i, 2, rows], s_y.at[i, 2 + way], dev(dy=1 + 2 * way))

    def y_pass(*offsets):
        for dz in offsets:
            i = RANK[dz]
            for way, rows in ((0, pl.ds(0, ah)), (1, pl.ds(ah, ah))):
                dy = 1 + 2 * way
                to = span(lax.rem(y + dy, 4))
                got(yb.at[i, 2, rows], s_y.at[i, 2 + way])
                dkp[i, rows, to] = (dkp[i, rows, to].astype(F32) + yb[i, 2, rows].astype(F32)).astype(BF16)
                send(dkp.at[i, pl.ds(0, a), to], yb.at[i, way], s_y.at[i, way], dev(dy=dy))

    def chain(dz, buf, sem, half):
        way = 0 if dz > 0 else 1
        left = abs(dz)
        if left == 3:
            rows = pl.ds(0, half) if dz > 0 else pl.ds(half, half)
        else:
            rows = pl.ds(0, 2 * half)
        got(buf.at[way, left, rows], sem.at[way, left])
        return way, left, rows

    def a_sum(dz):
        i = RANK[dz]
        for s in range(2):
            got(yb.at[i, s], s_y.at[i, s])
        return dkp[i, pl.ds(0, a), ycols].astype(F32) + (yb[i, 0].astype(F32) + yb[i, 1].astype(F32))

    def a_pass(dz):
        i = RANK[dz]
        dkp[i, pl.ds(0, a), ycols] = a_sum(dz).astype(BF16)
        if dz == 4:
            for way, rows in ((0, pl.ds(0, ah)), (1, pl.ds(ah, ah))):
                send(dkp.at[i, rows, ycols], za.at[way, 3, rows], s_za.at[way, 3], dev(dz=1 - 2 * way))
            return
        way, left, rows = chain(dz, za, s_za, ah)
        mine = dkp[i, rows, ycols].astype(F32) + za[way, left, rows].astype(F32)
        dkp[i, rows, ycols] = mine.astype(BF16)
        send(dkp.at[i, pl.ds(0, a), ycols], za.at[way, left - 1], s_za.at[way, left - 1], dev(dz=1 - 2 * way))

    def b_pass(dz):
        i = RANK[dz]
        if dz == 4:
            for way, rows in ((0, 0), (1, bh)):
                src = dkp.at[i, pl.ds(a + rows, bh)]
                send(src, zb.at[way, 3, pl.ds(rows, bh)], s_zb.at[way, 3], dev(dz=1 - 2 * way))
            return
        way, left, rows = chain(dz, zb, s_zb, bh)
        mine = pl.ds(a + rows.start, rows.size)
        dkp[i, mine] = (dkp[i, mine].astype(F32) + zb[way, left, rows].astype(F32)).astype(BF16)
        send(dkp.at[i, pl.ds(a, b)], zb.at[way, left - 1], s_zb.at[way, left - 1], dev(dz=1 - 2 * way))

    def query_part(d, s):
        zf = zl_of(d)
        j = zf * 2 + s
        keys = kb[pl.ds(pl.multiple_of((zf // 2) * 4, 4), 4), :, span(lax.rem(j, 4))]
        dqp[j] = (nn(wn[...], keys.reshape(1024, BLK)) * FACTOR).astype(BF16)
        to = 2 * s + c
        slot = lax.rem(x - to + 4, 4) - 1
        if s is xs:
            slot = jnp.maximum(slot, 0)
        send(
            dqp.at[j], rb.at[slot, zf], s_r.at[slot, zf], dev(x_to=to),
            when=jnp.logical_not(home) if s is xs else None,
        )

    def query_sum(d):
        zf = zl_of(d)
        j = zf * 2 + xs

        @pl.when(home)
        def _():
            for s in range(3):
                got(rb.at[s, zf], s_r.at[s, zf])
            total = (dqp[j].astype(F32) + rb[0, zf].astype(F32)) + (
                rb[1, zf].astype(F32) + rb[2, zf].astype(F32)
            )
            dqp[j] = total.astype(BF16)
            if d == 0:
                pltpu.make_async_copy(dqp.at[j, span(c)], oq_ref.at[span(zl)], s_own.at[1]).start()

        if d == 0:
            send(dqp.at[j, span(oc)], oq_ref.at[span(zl)], s_a.at[zl], partner, when=home)
        else:
            for r in (0, 1):
                send(dqp.at[j, span(r)], oq_ref.at[span(zl)], s_a.at[zl], dev(zl_to=zf, core=r), when=home)

    far = 1 - xs
    weights_of(0)
    key_part(4)
    b_pass(4)
    weights_of(3)
    key_part(3)
    weights_of(1)
    key_part(-3)
    weights_of(2)
    query_part(3, far)
    query_part(3, xs)
    y_pass(4)
    key_part(2)
    query_part(2, far)
    query_part(2, xs)
    b_pass(3)
    b_pass(-3)
    y_pass(3)
    key_part(-2)
    query_part(1, far)
    query_part(1, xs)
    y_pass(-3)
    key_part(1)
    query_part(0, far)
    query_part(0, xs)
    key_part(-1)
    a_pass(4)
    y_pass(2)
    key_part(0)
    b_pass(2)
    b_pass(-2)
    y_pass(-2)
    a_pass(3)
    a_pass(-3)
    y_pass(1)
    b_pass(1)
    b_pass(-1)
    query_sum(3)
    a_pass(2)
    a_pass(-2)
    y_pass(0)
    y_pass(-1)
    query_sum(2)
    for way in (0, 1):
        got(zb.at[way, 0], s_zb.at[way, 0])
    rest = dkp[0, pl.ds(a, b)].astype(F32) + (zb[0, 0].astype(F32) + zb[1, 0].astype(F32))
    dkp[0, pl.ds(a, b)] = rest.astype(BF16)
    for dy in (1, 3, 2):
        to = span(lax.rem(y + dy, 4))
        send(dkp.at[0, pl.ds(a, b), to], yb2.at[3 - dy], s_y2.at[3 - dy], dev(dy=dy))
    query_sum(1)
    a_pass(1)
    a_pass(-1)
    query_sum(0)
    total = a_sum(0)
    for s in range(3):
        got(yb2.at[s], s_y2.at[s])
    ok_ref[pl.ds(a, b), :] = (dkp[0, pl.ds(a, b), ycols].astype(F32) + yb2[0].astype(F32)) + (
        yb2[1].astype(F32) + yb2[2].astype(F32)
    )
    for d in (2, 1, 3):
        src = lax.rem(zl + d, 4)
        got(oq_ref.at[span(src)], s_a.at[src])
    mine = oq_ref.at[span(zl)]
    pl.when(away)(lambda: got(mine, s_a.at[zl]))
    pl.when(home)(lambda: pltpu.make_async_copy(mine, mine, s_own.at[1]).wait())

    for way in (0, 1):
        got(za.at[way, 0], s_za.at[way, 0])
    ok_ref[pl.ds(0, a), :] = total + (za[0, 0].astype(F32) + za[1, 0].astype(F32))

    for copy, when in sends:
        if when is None:
            copy.wait_send()
        else:
            pl.when(when)(copy.wait_send)


def widen(q_ref, k_ref, oq_ref, ok_ref):
    oq_ref[...] = q_ref[...].astype(F32)
    ok_ref[...] = k_ref[...]


def on_device(queries, keys, query_ids, memory_ids, target_gap, lse, counts):
    a = ZFIRST
    b = BLK - a
    vmem = pl.BlockSpec(memory_space=pltpu.VMEM)
    hbm = pl.BlockSpec(memory_space=pl.ANY)
    dma = pltpu.SemaphoreType.DMA
    query_grad, key_grad = pl.pallas_call(
        kernel,
        out_shape=(
            jax.ShapeDtypeStruct((1024, BLK), BF16),
            jax.ShapeDtypeStruct((BLK, BLK), F32),
        ),
        in_specs=[hbm] * 2 + [vmem] * 5,
        out_specs=(hbm, vmem),
        scratch_shapes=[
            pltpu.VMEM((512, 2048), BF16),
            pltpu.VMEM((8, BLK, 1024), BF16),
            pltpu.VMEM((4, 2, BLK, BLK), F32),
            pltpu.VMEM((4, BLK, BLK), F32),
            pltpu.VMEM((4, 8, BLK), jnp.int32),
            pltpu.VMEM((4, 8, BLK), F32),
            pltpu.VMEM((4, BLK, 512), BF16),
            pltpu.VMEM((512, 1024), BF16),
            pltpu.VMEM((8, BLK, 1024), BF16),
            pltpu.VMEM((8, 3, a, BLK), BF16),
            pltpu.VMEM((3, b, BLK), BF16),
            pltpu.VMEM((2, 4, a, BLK), BF16),
            pltpu.VMEM((2, 4, b, 1024), BF16),
            pltpu.VMEM((8, 512, BLK), BF16),
            pltpu.VMEM((3, 4, 512, BLK), BF16),
            dma((N_SENDS,)),
            dma((2,)),
            dma((9,)),
            dma((8, 4)),
            dma((9,)),
            dma((3,)),
            dma((8, 2)),
            dma((3,)),
            dma((4,)),
            dma((3,)),
            dma((4,)),
            dma((8, 4)),
            dma((3,)),
            dma((2, 4)),
            dma((2, 4)),
            dma((3, 4)),
            dma((4,)),
        ],
        compiler_params=pltpu.CompilerParams(
            collective_id=0, has_side_effects=True, vmem_limit_bytes=56 * 2**20
        ),
        cost_estimate=pl.CostEstimate(
            flops=6_442_450_944, bytes_accessed=3_000_000, transcendentals=262_144
        ),
        name="contrastive_backward",
    )(
        queries,
        keys,
        query_ids.reshape(1, -1),
        memory_ids.reshape(1, -1),
        target_gap.reshape(1, -1),
        lse.reshape(1, -1),
        counts.reshape(1, -1),
    )
    return pl.pallas_call(
        widen,
        out_shape=(
            jax.ShapeDtypeStruct((1024, BLK), F32),
            jax.ShapeDtypeStruct((BLK, BLK), F32),
        ),
        in_specs=[vmem] * 2,
        out_specs=(vmem, vmem),
        cost_estimate=pl.CostEstimate(flops=0, bytes_accessed=2_097_152, transcendentals=0),
        name="widen",
    )(query_grad, key_grad)


def solution(mesh):
    torus = Mesh(mesh.devices.reshape(2, 4, 2, 4, 4), AXES)
    return jax.shard_map(
        on_device,
        mesh=torus,
        in_specs=(P(PB, MA), P(MA, PB), P(PB), P(MA), P(PB), P(PB), P(PB)),
        out_specs=(P(PB, MA), P(MA, PB)),
        check_vma=False,
    )
```

```python
import math

import jax
import jax.numpy as jnp
from jax import lax
from jax.experimental import pallas as pl
from jax.experimental.pallas import tpu as pltpu
from jax.sharding import Mesh
from jax.sharding import PartitionSpec as P

D = 4096
GRAD_SCALE = 1024
AXES = ("zh", "y", "core", "zl", "x")
PB = ("zh", "y", "core")
MA = ("zl", "x")
FACTOR = 1.0 / math.sqrt(D)
BLK = 256
ZFIRST = 192
F32 = jnp.float32
BF16 = jnp.bfloat16
OFFSETS = (0, 1, -1, 2, -2, 3, -3, 4)
RANK = {dz: i for i, dz in enumerate(OFFSETS)}
N_SENDS = 89


def nt(a, b):
    return lax.dot_general(a, b, (((1,), (1,)), ((), ())), preferred_element_type=F32)


def nn(a, b):
    return jnp.dot(a, b, preferred_element_type=F32)


def kernel(
    q_ref, k_ref, qid_ref, mid_ref, gap_ref, lse_ref, cnt_ref, oq_ref, ok_ref,
    qb, kb, mk, st, sx, idb, mb, wt, wn, dkp, yb, yb2, za, zb, dqp, rb,
    ssem, s_own, s_kz, s_ky, s_bz, s_by, s_q, s_id, s_sx, s_m, s_w, s_y, s_y2, s_za, s_zb, s_r, s_a,
):
    zh, y, c, zl, x = [lax.axis_index(a) for a in AXES]
    z = zh * 4 + zl
    xp = lax.rem(x, 2)
    xs = x // 2
    home = xp == c
    oc = 1 - c
    a = ZFIRST
    ah = a // 2
    b = BLK - a
    bh = b // 2

    def zat(dz):
        return lax.rem(z + dz + 8, 8)

    def dev(dx=0, dy=0, dz=0, core=None, zl_to=None, x_to=None):
        zz = zat(dz)
        return (
            zz // 4,
            lax.rem(y + dy, 4),
            c if core is None else core,
            lax.rem(zz, 4) if zl_to is None else zl_to,
            lax.rem(x + dx, 4) if x_to is None else x_to,
        )

    def span(i, n=BLK):
        return pl.ds(pl.multiple_of(i * n, n), n)

    sends = []

    def send(src, dst, recv, to, when=None):
        copy = pltpu.make_async_remote_copy(
            src_ref=src,
            dst_ref=dst,
            send_sem=ssem.at[len(sends)],
            recv_sem=recv,
            device_id=to,
            device_id_type=pl.DeviceIdType.MESH,
        )
        if when is None:
            copy.start()
        else:
            pl.when(when)(copy.start)
        sends.append((copy, when))

    def drain():
        groups = {}
        for copy, when in sends:
            groups.setdefault(id(when), (when, []))[1].append(copy)
        for when, copies in groups.values():

            def wait_all(copies=copies):
                for copy in copies:
                    copy.wait_send()

            if when is None:
                wait_all()
            else:
                pl.when(when)(wait_all)
        sends.clear()

    partner = dev(core=oc)
    away = jnp.logical_not(home)

    def got(dst, recv):
        pltpu.make_async_remote_copy(
            src_ref=dst,
            dst_ref=dst,
            send_sem=ssem.at[0],
            recv_sem=recv,
            device_id=partner,
            device_id_type=pl.DeviceIdType.MESH,
        ).wait_recv()

    barrier = pltpu.get_barrier_semaphore()
    peers = [partner, dev(dz=1), dev(dz=-1)]
    for d in (1, 2, 3):
        other = lax.rem(zl + d, 4)
        peers += [dev(dx=d), dev(dy=d), dev(zl_to=other), dev(zl_to=other, core=oc)]
    for peer in peers:
        pl.semaphore_signal(barrier, inc=1, device_id=peer, device_id_type=pl.DeviceIdType.MESH)
    ycols = span(y)
    own_keys = pltpu.make_async_copy(k_ref, kb.at[z, :, ycols], s_own.at[0])
    own_keys.start()
    idb[zl] = jnp.broadcast_to(mid_ref[...], (8, BLK))
    pl.semaphore_wait(barrier, len(peers))

    def zslot(dz):
        return kb.at[zat(dz)]

    def a_block(dz, dy, rows):
        return kb.at[zat(dz), rows, span(lax.rem(y + dy, 4))]

    def a_z(dz, step, rows, part):
        blk = a_block(dz, 0, rows)
        to = dz - step
        i = 8 if part == 1 else RANK[4 if to == -4 else to]
        send(k_ref.at[rows] if dz == 0 else blk, blk, s_kz.at[i], dev(dz=step))

    def a_y(dz):
        blk = a_block(dz, 0, pl.ds(0, a))
        for dy in (1, 3):
            send(k_ref.at[pl.ds(0, a)] if dz == 0 else blk, blk, s_ky.at[RANK[dz], 3 - dy], dev(dy=dy))

    def a_relay(*offsets):
        for dz in offsets:
            i = RANK[dz]
            got(a_block(dz, 3, pl.ds(0, a)), s_ky.at[i, 2])
            blk = a_block(dz, 3, pl.ds(0, ah))
            send(blk, blk, s_ky.at[i, 1], dev(dy=1))
            got(a_block(dz, 1, pl.ds(0, a)), s_ky.at[i, 0])
            blk = a_block(dz, 1, pl.ds(ah, ah))
            send(blk, blk, s_ky.at[i, 3], dev(dy=3))

    def a_arrive(dz):
        for sign in (-1, 1) if dz < 4 else (0,):
            if dz == 4:
                got(a_block(4, 0, pl.ds(0, ah)), s_kz.at[7])
                got(a_block(4, 0, pl.ds(ah, ah)), s_kz.at[8])
                a_y(4)
                continue
            at = sign * dz
            got(a_block(at, 0, pl.ds(0, a)), s_kz.at[RANK[at]])
            if dz < 3:
                a_z(at, -sign, pl.ds(0, a), 0)
            elif sign < 0:
                a_z(at, 1, pl.ds(0, ah), 0)
            else:
                a_z(at, -1, pl.ds(ah, ah), 1)
        if dz < 4:
            a_y(-dz)
            a_y(dz)

    def b_z(dz, step, rows, part):
        blk = kb.at[zat(dz), rows]
        to = dz - step
        i = 8 if part == 1 else RANK[4 if to == -4 else to]
        send(blk, blk, s_bz.at[i], dev(dz=step))

    def b_arrive(dz):
        for sign in (-1, 1):
            at = sign * dz
            got(kb.at[zat(at), pl.ds(a, b)], s_bz.at[RANK[at]])
            if dz < 3:
                b_z(at, -sign, pl.ds(a, b), 0)
            elif sign < 0:
                b_z(at, 1, pl.ds(a, bh), 0)
            else:
                b_z(at, -1, pl.ds(a + bh, bh), 1)

    def q_block(j, r):
        return qb.at[span(r), span(j)]

    def zl_of(d):
        return (zl, zl + 1 - 2 * lax.rem(zl, 2), lax.rem(zl + 2, 4), 3 - zl)[d]

    j_own = zl * 2 + xs
    for d in (1, 2, 3):
        send(idb.at[zl], idb.at[zl], s_id.at[3 - d], dev(zl_to=lax.rem(zl + d, 4)))
    send(q_ref.at[span(zl)], q_block(j_own, c), s_q.at[j_own, c], dev(core=xp), when=away)

    def q_exchange(d):
        to = zl_of(d)
        send(q_ref.at[span(to)], q_block(j_own, c), s_q.at[j_own, c], dev(zl_to=to, core=xp))

    own_queries = pltpu.make_async_copy(q_ref.at[span(zl)], q_block(j_own, c), s_own.at[1])
    pl.when(home)(own_queries.start)

    def q_spread(j, r, own=False):
        if not own:
            pl.when(home)(lambda: got(q_block(j, r), s_q.at[j, r]))
        src = q_ref.at[span(zl)] if own else q_block(j, r)
        for dx in (1, 3):
            send(src, q_block(j, r), s_q.at[j, r], dev(dx=dx), when=home)

    def q_arrive(d):
        j = zl_of(d) * 2 + xs
        q_spread(j, 0)
        q_spread(j, 1)

    def q_from(dx, d):
        return zl_of(d) * 2 + lax.rem(x + dx, 4) // 2

    def q_relay(d):
        for r, dx in ((0, 3), (1, 1)):
            blk = q_block(q_from(dx, d), r)
            sem = s_q.at[q_from(dx, d), r]
            pl.when(away)(lambda: got(blk, sem))
            send(blk, blk, sem, dev(dx=4 - dx), when=away)

    qrow = span(zl)
    qid = qid_ref[:, qrow].astype(F32)
    lse = lse_ref[:, qrow]

    def matches():
        for d in (0, 1, 2, 3):
            m = lax.rem(zl + d, 4)
            if d > 0:
                got(idb.at[m], s_id.at[d - 1])
            ids = jnp.broadcast_to(idb[m][0:1, :].astype(F32), (128, BLK)).T
            mk[m] = (ids[:, 0:1] == qid).astype(F32)

    def scores(dz, last):
        i = RANK[dz]
        got(a_block(dz, 2, pl.ds(0, ah)), s_ky.at[i, 1])
        got(a_block(dz, 2, pl.ds(ah, ah)), s_ky.at[i, 3])
        if dz == 4:
            got(kb.at[zat(4), pl.ds(a, bh)], s_bz.at[7])
            got(kb.at[zat(4), pl.ds(a + bh, bh)], s_bz.at[8])
        m = lax.rem(zat(dz), 4)
        part = zat(dz) // 4
        for r in (oc, c):
            s = nt(kb[zat(dz)], qb[span(r), span(part, 1024)])
            st[m, r] = st[m, r] + s if last else s
            if last and r is oc:
                send(st.at[m, oc], sx.at[m], s_sx.at[m], partner)

    def probs(dz):
        m = lax.rem(zat(dz), 4)
        got(sx.at[m], s_sx.at[m])
        p = jnp.exp((st[m, c] + sx[m]) * FACTOR - lse)
        st[m, c] = p
        return jnp.sum(mk[m] * p, axis=0, keepdims=True)

    a_z(0, 1, pl.ds(0, a), 0)
    a_z(0, -1, pl.ds(0, a), 0)
    a_y(0)
    q_spread(j_own, c, own=True)
    q_spread(j_own, oc)
    pl.when(home)(own_queries.wait)
    q_exchange(3)
    for dy in (1, 3, 2):
        send(k_ref.at[pl.ds(a, b)], a_block(0, 0, pl.ds(a, b)), s_by.at[3 - dy], dev(dy=dy))
    a_arrive(1)
    q_exchange(1)
    q_exchange(2)
    a_relay(0)
    a_relay(1)
    own_keys.wait()
    for dy in (1, 3, 2):
        got(a_block(0, 4 - dy, pl.ds(a, b)), s_by.at[3 - dy])
    b_z(0, 1, pl.ds(a, b), 0)
    b_z(0, -1, pl.ds(a, b), 0)
    q_relay(0)
    q_arrive(3)
    q_arrive(1)
    a_arrive(2)
    q_arrive(2)
    matches()
    b_arrive(1)
    q_relay(1)
    a_relay(-1)
    a_arrive(3)
    b_arrive(2)
    a_arrive(4)
    a_relay(2)
    q_relay(3)
    q_relay(2)
    b_arrive(3)
    a_relay(-2)
    a_relay(3)
    a_relay(-3)
    @pl.when(home)
    def _():
        for d in (0, 1, 2, 3):
            for r in (0, 1):
                j = zl_of(d) * 2 + (1 - xs)
                got(q_block(j, r), s_q.at[j, r])

    @pl.when(away)
    def _():
        for d in (0, 1, 2, 3):
            for r, dx in ((1, 3), (0, 1)):
                j = q_from(dx, d)
                got(q_block(j, r), s_q.at[j, r])

    scores(0, False)
    scores(1, False)
    a_relay(4)
    scores(-1, False)
    scores(2, False)
    scores(-2, True)
    scores(3, True)
    matched = probs(-2)
    scores(-3, True)
    matched = matched + probs(3)
    scores(4, True)
    matched = matched + probs(-3)
    matched = matched + probs(4)

    mb[0] = jnp.broadcast_to(matched, (8, BLK))
    for d in (1, 3, 2):
        send(mb.at[0], mb.at[4 - d], s_m.at[3 - d], dev(dx=d))
    scale = jnp.float32(GRAD_SCALE) / cnt_ref[:, qrow].astype(F32)
    gap = jnp.exp(gap_ref[:, qrow])
    drain()
    for d in (1, 3, 2):
        got(mb.at[4 - d], s_m.at[3 - d])
    positive = gap + ((mb[0] + mb[1]) + (mb[2] + mb[3]))[0:1, :]
    inverse = 1.0 / positive

    def weigh(d):
        m = lax.rem(zl + d, 4)
        p = st[m, c]
        st[m, c] = (p - mk[m] * p * inverse) * scale
        wt[m, :, span(c)] = st[m, c].astype(BF16)
        blk = wt.at[m, :, span(c)]
        send(blk, blk, s_w.at[m], partner)

    def weights_of(d):
        m = lax.rem(zl + d, 4)
        got(wt.at[m, :, span(oc)], s_w.at[m])

    def turn(d):
        m = lax.rem(zl + d, 4)
        wn[span(c), span(m)] = st[m, c].T.astype(BF16)
        wn[span(oc), span(m)] = wt[m, :, span(oc)].astype(F32).T.astype(BF16)

    def key_part(dz):
        i = RANK[dz]
        m = lax.rem(zat(dz), 4)
        part = zat(dz) // 4
        dkp[i] = (nn(wt[m], qb[:, span(part, 1024)]) * FACTOR).astype(BF16)
        far = span(lax.rem(y + 2, 4))
        for way, rows in ((0, pl.ds(0, ah)), (1, pl.ds(ah, ah))):
            send(dkp.at[i, rows, far], yb.at[i, 2, rows], s_y.at[i, 2 + way], dev(dy=1 + 2 * way))

    def y_pass(*offsets):
        for dz in offsets:
            i = RANK[dz]
            for way, rows in ((0, pl.ds(0, ah)), (1, pl.ds(ah, ah))):
                dy = 1 + 2 * way
                to = span(lax.rem(y + dy, 4))
                got(yb.at[i, 2, rows], s_y.at[i, 2 + way])
                dkp[i, rows, to] = (dkp[i, rows, to].astype(F32) + yb[i, 2, rows].astype(F32)).astype(BF16)
                send(dkp.at[i, pl.ds(0, a), to], yb.at[i, way], s_y.at[i, way], dev(dy=dy))

    def chain(dz, buf, sem, half):
        way = 0 if dz > 0 else 1
        left = abs(dz)
        if left == 3:
            rows = pl.ds(0, half) if dz > 0 else pl.ds(half, half)
        else:
            rows = pl.ds(0, 2 * half)
        got(buf.at[way, left, rows], sem.at[way, left])
        return way, left, rows

    def a_sum(dz):
        i = RANK[dz]
        for s in range(2):
            got(yb.at[i, s], s_y.at[i, s])
        return dkp[i, pl.ds(0, a), ycols].astype(F32) + (yb[i, 0].astype(F32) + yb[i, 1].astype(F32))

    def a_pass(dz):
        i = RANK[dz]
        dkp[i, pl.ds(0, a), ycols] = a_sum(dz).astype(BF16)
        if dz == 4:
            for way, rows in ((0, pl.ds(0, ah)), (1, pl.ds(ah, ah))):
                send(dkp.at[i, rows, ycols], za.at[way, 3, rows], s_za.at[way, 3], dev(dz=1 - 2 * way))
            return
        way, left, rows = chain(dz, za, s_za, ah)
        mine = dkp[i, rows, ycols].astype(F32) + za[way, left, rows].astype(F32)
        dkp[i, rows, ycols] = mine.astype(BF16)
        send(dkp.at[i, pl.ds(0, a), ycols], za.at[way, left - 1], s_za.at[way, left - 1], dev(dz=1 - 2 * way))

    def b_pass(dz):
        i = RANK[dz]
        if dz == 4:
            for way, rows in ((0, 0), (1, bh)):
                src = dkp.at[i, pl.ds(a + rows, bh)]
                send(src, zb.at[way, 3, pl.ds(rows, bh)], s_zb.at[way, 3], dev(dz=1 - 2 * way))
            return
        way, left, rows = chain(dz, zb, s_zb, bh)
        mine = pl.ds(a + rows.start, rows.size)
        dkp[i, mine] = (dkp[i, mine].astype(F32) + zb[way, left, rows].astype(F32)).astype(BF16)
        send(dkp.at[i, pl.ds(a, b)], zb.at[way, left - 1], s_zb.at[way, left - 1], dev(dz=1 - 2 * way))

    def query_part(d, s):
        zf = zl_of(d)
        j = zf * 2 + s
        keys = kb[pl.ds(pl.multiple_of((zf // 2) * 4, 4), 4), :, span(lax.rem(j, 4))]
        dqp[j] = (nn(wn[...], keys.reshape(1024, BLK)) * FACTOR).astype(BF16)
        to = 2 * s + c
        slot = lax.rem(x - to + 4, 4) - 1
        if s is xs:
            slot = jnp.maximum(slot, 0)
        send(
            dqp.at[j], rb.at[slot, zf], s_r.at[slot, zf], dev(x_to=to),
            when=away if s is xs else None,
        )

    def query_sum(d):
        zf = zl_of(d)
        j = zf * 2 + xs

        @pl.when(home)
        def _():
            for s in range(3):
                got(rb.at[s, zf], s_r.at[s, zf])
            total = (dqp[j].astype(F32) + rb[0, zf].astype(F32)) + (
                rb[1, zf].astype(F32) + rb[2, zf].astype(F32)
            )
            dqp[j] = total.astype(BF16)
            if d == 0:
                pltpu.make_async_copy(dqp.at[j, span(c)], oq_ref.at[span(zl)], s_own.at[1]).start()

        if d == 0:
            send(dqp.at[j, span(oc)], oq_ref.at[span(zl)], s_a.at[zl], partner, when=home)
        else:
            for r in (0, 1):
                send(dqp.at[j, span(r)], oq_ref.at[span(zl)], s_a.at[zl], dev(zl_to=zf, core=r), when=home)

    far = 1 - xs
    weigh(0)
    weigh(3)
    weights_of(0)
    key_part(4)
    b_pass(4)
    weigh(1)
    weights_of(3)
    key_part(3)
    weigh(2)
    weights_of(1)
    key_part(-3)
    weights_of(2)
    for d in (0, 3, 1, 2):
        turn(d)
    query_part(3, far)
    query_part(3, xs)
    y_pass(4)
    key_part(2)
    query_part(2, far)
    query_part(2, xs)
    b_pass(3)
    b_pass(-3)
    y_pass(3)
    key_part(-2)
    query_part(1, far)
    query_part(1, xs)
    y_pass(-3)
    key_part(1)
    query_part(0, far)
    query_part(0, xs)
    key_part(-1)
    a_pass(4)
    y_pass(2)
    key_part(0)
    b_pass(2)
    b_pass(-2)
    y_pass(-2)
    a_pass(3)
    a_pass(-3)
    y_pass(1)
    b_pass(1)
    b_pass(-1)
    query_sum(3)
    a_pass(2)
    a_pass(-2)
    y_pass(0)
    y_pass(-1)
    query_sum(2)
    for way in (0, 1):
        got(zb.at[way, 0], s_zb.at[way, 0])
    rest = dkp[0, pl.ds(a, b)].astype(F32) + (zb[0, 0].astype(F32) + zb[1, 0].astype(F32))
    dkp[0, pl.ds(a, b)] = rest.astype(BF16)
    for dy in (1, 3, 2):
        to = span(lax.rem(y + dy, 4))
        send(dkp.at[0, pl.ds(a, b), to], yb2.at[3 - dy], s_y2.at[3 - dy], dev(dy=dy))
    query_sum(1)
    a_pass(1)
    a_pass(-1)
    query_sum(0)
    total = a_sum(0)
    for s in range(3):
        got(yb2.at[s], s_y2.at[s])
    ok_ref[pl.ds(a, b), :] = (dkp[0, pl.ds(a, b), ycols].astype(F32) + yb2[0].astype(F32)) + (
        yb2[1].astype(F32) + yb2[2].astype(F32)
    )
    for d in (2, 1, 3):
        src = lax.rem(zl + d, 4)
        got(oq_ref.at[span(src)], s_a.at[src])
    mine = oq_ref.at[span(zl)]
    pl.when(away)(lambda: got(mine, s_a.at[zl]))
    pl.when(home)(lambda: pltpu.make_async_copy(mine, mine, s_own.at[1]).wait())

    for way in (0, 1):
        got(za.at[way, 0], s_za.at[way, 0])
    drain()
    ok_ref[pl.ds(0, a), :] = total + (za[0, 0].astype(F32) + za[1, 0].astype(F32))


def widen(q_ref, k_ref, oq_ref, ok_ref):
    oq_ref[...] = q_ref[...].astype(F32)
    ok_ref[...] = k_ref[...]


def on_device(queries, keys, query_ids, memory_ids, target_gap, lse, counts):
    a = ZFIRST
    b = BLK - a
    vmem = pl.BlockSpec(memory_space=pltpu.VMEM)
    hbm = pl.BlockSpec(memory_space=pl.ANY)
    dma = pltpu.SemaphoreType.DMA
    query_grad, key_grad = pl.pallas_call(
        kernel,
        out_shape=(
            jax.ShapeDtypeStruct((1024, BLK), BF16),
            jax.ShapeDtypeStruct((BLK, BLK), F32),
        ),
        in_specs=[hbm] * 2 + [vmem] * 5,
        out_specs=(hbm, vmem),
        scratch_shapes=[
            pltpu.VMEM((512, 2048), BF16),
            pltpu.VMEM((8, BLK, 1024), BF16),
            pltpu.VMEM((4, BLK, BLK), F32),
            pltpu.VMEM((4, 2, BLK, BLK), F32),
            pltpu.VMEM((4, BLK, BLK), F32),
            pltpu.VMEM((4, 8, BLK), jnp.int32),
            pltpu.VMEM((4, 8, BLK), F32),
            pltpu.VMEM((4, BLK, 512), BF16),
            pltpu.VMEM((512, 1024), BF16),
            pltpu.VMEM((8, BLK, 1024), BF16),
            pltpu.VMEM((8, 3, a, BLK), BF16),
            pltpu.VMEM((3, b, BLK), BF16),
            pltpu.VMEM((2, 4, a, BLK), BF16),
            pltpu.VMEM((2, 4, b, 1024), BF16),
            pltpu.VMEM((8, 512, BLK), BF16),
            pltpu.VMEM((3, 4, 512, BLK), BF16),
            dma((N_SENDS,)),
            dma((2,)),
            dma((9,)),
            dma((8, 4)),
            dma((9,)),
            dma((3,)),
            dma((8, 2)),
            dma((3,)),
            dma((4,)),
            dma((3,)),
            dma((4,)),
            dma((8, 4)),
            dma((3,)),
            dma((2, 4)),
            dma((2, 4)),
            dma((3, 4)),
            dma((4,)),
        ],
        compiler_params=pltpu.CompilerParams(
            collective_id=0, has_side_effects=True, vmem_limit_bytes=56 * 2**20
        ),
        cost_estimate=pl.CostEstimate(
            flops=6_442_450_944, bytes_accessed=3_000_000, transcendentals=262_144
        ),
        name="contrastive_backward",
    )(
        queries,
        keys,
        query_ids.reshape(1, -1),
        memory_ids.reshape(1, -1),
        target_gap.reshape(1, -1),
        lse.reshape(1, -1),
        counts.reshape(1, -1),
    )
    return pl.pallas_call(
        widen,
        out_shape=(
            jax.ShapeDtypeStruct((1024, BLK), F32),
            jax.ShapeDtypeStruct((BLK, BLK), F32),
        ),
        in_specs=[vmem] * 2,
        out_specs=(vmem, vmem),
        cost_estimate=pl.CostEstimate(flops=0, bytes_accessed=2_097_152, transcendentals=0),
        name="widen",
    )(query_grad, key_grad)


def solution(mesh):
    torus = Mesh(mesh.devices.reshape(2, 4, 2, 4, 4), AXES)
    return jax.shard_map(
        on_device,
        mesh=torus,
        in_specs=(P(PB, MA), P(MA, PB), P(PB), P(MA), P(PB), P(PB), P(PB)),
        out_specs=(P(PB, MA), P(MA, PB)),
        check_vma=False,
    )
```

```python
import math

import jax
import jax.numpy as jnp
from jax import lax
from jax.experimental import pallas as pl
from jax.experimental.pallas import tpu as pltpu
from jax.sharding import Mesh
from jax.sharding import PartitionSpec as P

D = 4096
GRAD_SCALE = 1024
AXES = ("zh", "y", "core", "zl", "x")
PB = ("zh", "y", "core")
MA = ("zl", "x")
FACTOR = 1.0 / math.sqrt(D)
BLK = 256
ZFIRST = 192
F32 = jnp.float32
BF16 = jnp.bfloat16
OFFSETS = (0, 1, -1, 2, -2, 3, -3, 4)
RANK = {dz: i for i, dz in enumerate(OFFSETS)}
N_SENDS = 89


def nt(a, b):
    return lax.dot_general(a, b, (((1,), (1,)), ((), ())), preferred_element_type=F32)


def nn(a, b):
    return jnp.dot(a, b, preferred_element_type=F32)


def kernel(
    q_ref, k_ref, qid_ref, mid_ref, gap_ref, lse_ref, cnt_ref, oq_ref, ok_ref,
    qb, kb, mk, st, sx, idb, mb, wt, wn, dkp, yb, yb2, za, zb, dqp, rb,
    ssem, s_own, s_kz, s_ky, s_bz, s_by, s_q, s_id, s_sx, s_m, s_w, s_y, s_y2, s_za, s_zb, s_r, s_a,
):
    zh, y, c, zl, x = [lax.axis_index(a) for a in AXES]
    z = zh * 4 + zl
    xp = lax.rem(x, 2)
    xs = x // 2
    home = xp == c
    oc = 1 - c
    a = ZFIRST
    ah = a // 2
    b = BLK - a
    bh = b // 2

    def zat(dz):
        return lax.rem(z + dz + 8, 8)

    def dev(dx=0, dy=0, dz=0, core=None, zl_to=None, x_to=None):
        zz = zat(dz)
        return (
            zz // 4,
            lax.rem(y + dy, 4),
            c if core is None else core,
            lax.rem(zz, 4) if zl_to is None else zl_to,
            lax.rem(x + dx, 4) if x_to is None else x_to,
        )

    def span(i, n=BLK):
        return pl.ds(pl.multiple_of(i * n, n), n)

    sends = []

    def send(src, dst, recv, to, when=None):
        copy = pltpu.make_async_remote_copy(
            src_ref=src,
            dst_ref=dst,
            send_sem=ssem.at[len(sends)],
            recv_sem=recv,
            device_id=to,
            device_id_type=pl.DeviceIdType.MESH,
        )
        if when is None:
            copy.start()
        else:
            pl.when(when)(copy.start)
        sends.append((copy, when))

    def drain():
        groups = {}
        for copy, when in sends:
            groups.setdefault(id(when), (when, []))[1].append(copy)
        for when, copies in groups.values():

            def wait_all(copies=copies):
                for copy in copies:
                    copy.wait_send()

            if when is None:
                wait_all()
            else:
                pl.when(when)(wait_all)
        sends.clear()

    partner = dev(core=oc)
    away = jnp.logical_not(home)

    def got(dst, recv):
        pltpu.make_async_remote_copy(
            src_ref=dst,
            dst_ref=dst,
            send_sem=ssem.at[0],
            recv_sem=recv,
            device_id=partner,
            device_id_type=pl.DeviceIdType.MESH,
        ).wait_recv()

    barrier = pltpu.get_barrier_semaphore()
    peers = [partner, dev(dz=1), dev(dz=-1)]
    for d in (1, 2, 3):
        other = lax.rem(zl + d, 4)
        peers += [dev(dx=d), dev(dy=d), dev(zl_to=other), dev(zl_to=other, core=oc)]
    for peer in peers:
        pl.semaphore_signal(barrier, inc=1, device_id=peer, device_id_type=pl.DeviceIdType.MESH)
    ycols = span(y)
    own_keys = pltpu.make_async_copy(k_ref, kb.at[z, :, ycols], s_own.at[0])
    own_keys.start()
    idb[zl] = jnp.broadcast_to(mid_ref[...], (8, BLK))
    pl.semaphore_wait(barrier, len(peers))

    def zslot(dz):
        return kb.at[zat(dz)]

    def a_block(dz, dy, rows):
        return kb.at[zat(dz), rows, span(lax.rem(y + dy, 4))]

    def a_z(dz, step, rows, part):
        blk = a_block(dz, 0, rows)
        to = dz - step
        i = 8 if part == 1 else RANK[4 if to == -4 else to]
        send(k_ref.at[rows] if dz == 0 else blk, blk, s_kz.at[i], dev(dz=step))

    def a_y(dz):
        blk = a_block(dz, 0, pl.ds(0, a))
        for dy in (1, 3):
            send(k_ref.at[pl.ds(0, a)] if dz == 0 else blk, blk, s_ky.at[RANK[dz], 3 - dy], dev(dy=dy))

    def a_relay(*offsets):
        for dz in offsets:
            i = RANK[dz]
            got(a_block(dz, 3, pl.ds(0, a)), s_ky.at[i, 2])
            blk = a_block(dz, 3, pl.ds(0, ah))
            send(blk, blk, s_ky.at[i, 1], dev(dy=1))
            got(a_block(dz, 1, pl.ds(0, a)), s_ky.at[i, 0])
            blk = a_block(dz, 1, pl.ds(ah, ah))
            send(blk, blk, s_ky.at[i, 3], dev(dy=3))

    def a_arrive(dz):
        for sign in (-1, 1) if dz < 4 else (0,):
            if dz == 4:
                got(a_block(4, 0, pl.ds(0, ah)), s_kz.at[7])
                got(a_block(4, 0, pl.ds(ah, ah)), s_kz.at[8])
                a_y(4)
                continue
            at = sign * dz
            got(a_block(at, 0, pl.ds(0, a)), s_kz.at[RANK[at]])
            if dz < 3:
                a_z(at, -sign, pl.ds(0, a), 0)
            elif sign < 0:
                a_z(at, 1, pl.ds(0, ah), 0)
            else:
                a_z(at, -1, pl.ds(ah, ah), 1)
        if dz < 4:
            a_y(-dz)
            a_y(dz)

    def b_z(dz, step, rows, part):
        blk = kb.at[zat(dz), rows]
        to = dz - step
        i = 8 if part == 1 else RANK[4 if to == -4 else to]
        send(blk, blk, s_bz.at[i], dev(dz=step))

    def b_arrive(dz):
        for sign in (-1, 1):
            at = sign * dz
            got(kb.at[zat(at), pl.ds(a, b)], s_bz.at[RANK[at]])
            if dz < 3:
                b_z(at, -sign, pl.ds(a, b), 0)
            elif sign < 0:
                b_z(at, 1, pl.ds(a, bh), 0)
            else:
                b_z(at, -1, pl.ds(a + bh, bh), 1)

    def q_block(j, r):
        return qb.at[span(r), span(j)]

    def zl_of(d):
        return (zl, zl + 1 - 2 * lax.rem(zl, 2), lax.rem(zl + 2, 4), 3 - zl)[d]

    j_own = zl * 2 + xs
    for d in (1, 2, 3):
        send(idb.at[zl], idb.at[zl], s_id.at[3 - d], dev(zl_to=lax.rem(zl + d, 4)))
    send(q_ref.at[span(zl)], q_block(j_own, c), s_q.at[j_own, c], dev(core=xp), when=away)

    def q_exchange(d):
        to = zl_of(d)
        send(q_ref.at[span(to)], q_block(j_own, c), s_q.at[j_own, c], dev(zl_to=to, core=xp))

    own_queries = pltpu.make_async_copy(q_ref.at[span(zl)], q_block(j_own, c), s_own.at[1])
    pl.when(home)(own_queries.start)

    def q_spread(j, r, own=False):
        if not own:
            pl.when(home)(lambda: got(q_block(j, r), s_q.at[j, r]))
        src = q_ref.at[span(zl)] if own else q_block(j, r)
        for dx in (1, 3):
            send(src, q_block(j, r), s_q.at[j, r], dev(dx=dx), when=home)

    def q_arrive(d):
        j = zl_of(d) * 2 + xs
        q_spread(j, 0)
        q_spread(j, 1)

    def q_from(dx, d):
        return zl_of(d) * 2 + lax.rem(x + dx, 4) // 2

    def q_relay(d):
        for r, dx in ((0, 3), (1, 1)):
            blk = q_block(q_from(dx, d), r)
            sem = s_q.at[q_from(dx, d), r]
            pl.when(away)(lambda: got(blk, sem))
            send(blk, blk, sem, dev(dx=4 - dx), when=away)

    qrow = span(zl)
    qid = qid_ref[:, qrow].astype(F32)
    lse = lse_ref[:, qrow]

    def matches():
        for d in (0, 1, 2, 3):
            m = lax.rem(zl + d, 4)
            if d > 0:
                got(idb.at[m], s_id.at[d - 1])
            ids = jnp.broadcast_to(idb[m][0:1, :].astype(F32), (128, BLK)).T
            mk[m] = (ids[:, 0:1] == qid).astype(F32)

    def scores(dz, last):
        i = RANK[dz]
        got(a_block(dz, 2, pl.ds(0, ah)), s_ky.at[i, 1])
        got(a_block(dz, 2, pl.ds(ah, ah)), s_ky.at[i, 3])
        if dz == 4:
            got(kb.at[zat(4), pl.ds(a, bh)], s_bz.at[7])
            got(kb.at[zat(4), pl.ds(a + bh, bh)], s_bz.at[8])
        m = lax.rem(zat(dz), 4)
        part = zat(dz) // 4
        for r in (oc, c):
            s = nt(kb[zat(dz)], qb[span(r), span(part, 1024)])
            st[m, r] = st[m, r] + s if last else s
            if last and r is oc:
                send(st.at[m, oc], sx.at[m], s_sx.at[m], partner)

    def probs(dz):
        m = lax.rem(zat(dz), 4)
        got(sx.at[m], s_sx.at[m])
        p = jnp.exp((st[m, c] + sx[m]) * FACTOR - lse)
        st[m, c] = p
        return jnp.sum(mk[m] * p, axis=0, keepdims=True)

    a_z(0, 1, pl.ds(0, a), 0)
    a_z(0, -1, pl.ds(0, a), 0)
    a_y(0)
    q_spread(j_own, c, own=True)
    q_spread(j_own, oc)
    pl.when(home)(own_queries.wait)
    q_exchange(3)
    for dy in (1, 3, 2):
        send(k_ref.at[pl.ds(a, b)], a_block(0, 0, pl.ds(a, b)), s_by.at[3 - dy], dev(dy=dy))
    a_arrive(1)
    q_exchange(1)
    q_exchange(2)
    a_relay(0)
    a_relay(1)
    own_keys.wait()
    for dy in (1, 3, 2):
        got(a_block(0, 4 - dy, pl.ds(a, b)), s_by.at[3 - dy])
    b_z(0, 1, pl.ds(a, b), 0)
    b_z(0, -1, pl.ds(a, b), 0)
    q_relay(0)
    q_arrive(3)
    q_arrive(1)
    a_arrive(2)
    q_arrive(2)
    matches()
    b_arrive(1)
    q_relay(1)
    a_relay(-1)
    a_arrive(3)
    b_arrive(2)
    a_arrive(4)
    a_relay(2)
    q_relay(3)
    q_relay(2)
    b_arrive(3)
    a_relay(-2)
    a_relay(3)
    a_relay(-3)
    @pl.when(home)
    def _():
        for d in (0, 1, 2, 3):
            for r in (0, 1):
                j = zl_of(d) * 2 + (1 - xs)
                got(q_block(j, r), s_q.at[j, r])

    @pl.when(away)
    def _():
        for d in (0, 1, 2, 3):
            for r, dx in ((1, 3), (0, 1)):
                j = q_from(dx, d)
                got(q_block(j, r), s_q.at[j, r])

    scores(0, False)
    scores(1, False)
    a_relay(4)
    scores(-1, False)
    scores(2, False)
    scores(-2, True)
    scores(3, True)
    matched = probs(-2)
    scores(-3, True)
    matched = matched + probs(3)
    scores(4, True)
    matched = matched + probs(-3)
    matched = matched + probs(4)

    mb[0] = jnp.broadcast_to(matched, (8, BLK))
    for d in (1, 3, 2):
        send(mb.at[0], mb.at[4 - d], s_m.at[3 - d], dev(dx=d))
    scale = jnp.float32(GRAD_SCALE) / cnt_ref[:, qrow].astype(F32)
    gap = jnp.exp(gap_ref[:, qrow])
    drain()
    for d in (1, 3, 2):
        got(mb.at[4 - d], s_m.at[3 - d])
    positive = gap + ((mb[0] + mb[1]) + (mb[2] + mb[3]))[0:1, :]
    inverse = 1.0 / positive

    def weigh(d):
        m = lax.rem(zl + d, 4)
        p = st[m, c]
        st[m, c] = (p - mk[m] * p * inverse) * scale
        wt[m, :, span(c)] = st[m, c].astype(BF16)
        blk = wt.at[m, :, span(c)]
        send(blk, blk, s_w.at[m], partner)

    def weights_of(d):
        m = lax.rem(zl + d, 4)
        got(wt.at[m, :, span(oc)], s_w.at[m])

    def turn(d):
        m = lax.rem(zl + d, 4)
        wn[span(c), span(m)] = st[m, c].T.astype(BF16)
        wn[span(oc), span(m)] = wt[m, :, span(oc)].astype(F32).T.astype(BF16)

    def key_part(dz):
        i = RANK[dz]
        m = lax.rem(zat(dz), 4)
        part = zat(dz) // 4
        for dy in (2, 1, 3, 0):
            col = lax.rem(y + dy, 4)
            block = nn(wt[m], qb[:, span(part * 4 + col)])
            dkp[i, :, span(col)] = (block * FACTOR).astype(BF16)
            if dy == 2:
                for way, rows in ((0, pl.ds(0, ah)), (1, pl.ds(ah, ah))):
                    src = dkp.at[i, rows, span(col)]
                    send(src, yb.at[i, 2, rows], s_y.at[i, 2 + way], dev(dy=1 + 2 * way))

    def y_pass(*offsets):
        for dz in offsets:
            i = RANK[dz]
            for way, rows in ((0, pl.ds(0, ah)), (1, pl.ds(ah, ah))):
                dy = 1 + 2 * way
                to = span(lax.rem(y + dy, 4))
                got(yb.at[i, 2, rows], s_y.at[i, 2 + way])
                dkp[i, rows, to] = (dkp[i, rows, to].astype(F32) + yb[i, 2, rows].astype(F32)).astype(BF16)
                send(dkp.at[i, pl.ds(0, a), to], yb.at[i, way], s_y.at[i, way], dev(dy=dy))

    def chain(dz, buf, sem, half):
        way = 0 if dz > 0 else 1
        left = abs(dz)
        if left == 3:
            rows = pl.ds(0, half) if dz > 0 else pl.ds(half, half)
        else:
            rows = pl.ds(0, 2 * half)
        got(buf.at[way, left, rows], sem.at[way, left])
        return way, left, rows

    def a_sum(dz):
        i = RANK[dz]
        for s in range(2):
            got(yb.at[i, s], s_y.at[i, s])
        return dkp[i, pl.ds(0, a), ycols].astype(F32) + (yb[i, 0].astype(F32) + yb[i, 1].astype(F32))

    def a_pass(dz):
        i = RANK[dz]
        dkp[i, pl.ds(0, a), ycols] = a_sum(dz).astype(BF16)
        if dz == 4:
            for way, rows in ((0, pl.ds(0, ah)), (1, pl.ds(ah, ah))):
                send(dkp.at[i, rows, ycols], za.at[way, 3, rows], s_za.at[way, 3], dev(dz=1 - 2 * way))
            return
        way, left, rows = chain(dz, za, s_za, ah)
        mine = dkp[i, rows, ycols].astype(F32) + za[way, left, rows].astype(F32)
        dkp[i, rows, ycols] = mine.astype(BF16)
        send(dkp.at[i, pl.ds(0, a), ycols], za.at[way, left - 1], s_za.at[way, left - 1], dev(dz=1 - 2 * way))

    def b_pass(dz):
        i = RANK[dz]
        if dz == 4:
            for way, rows in ((0, 0), (1, bh)):
                src = dkp.at[i, pl.ds(a + rows, bh)]
                send(src, zb.at[way, 3, pl.ds(rows, bh)], s_zb.at[way, 3], dev(dz=1 - 2 * way))
            return
        way, left, rows = chain(dz, zb, s_zb, bh)
        mine = pl.ds(a + rows.start, rows.size)
        dkp[i, mine] = (dkp[i, mine].astype(F32) + zb[way, left, rows].astype(F32)).astype(BF16)
        send(dkp.at[i, pl.ds(a, b)], zb.at[way, left - 1], s_zb.at[way, left - 1], dev(dz=1 - 2 * way))

    def query_part(d, s):
        zf = zl_of(d)
        j = zf * 2 + s
        keys = kb[pl.ds(pl.multiple_of((zf // 2) * 4, 4), 4), :, span(lax.rem(j, 4))]
        dqp[j] = (nn(wn[...], keys.reshape(1024, BLK)) * FACTOR).astype(BF16)
        to = 2 * s + c
        slot = lax.rem(x - to + 4, 4) - 1
        if s is xs:
            slot = jnp.maximum(slot, 0)
        send(
            dqp.at[j], rb.at[slot, zf], s_r.at[slot, zf], dev(x_to=to),
            when=away if s is xs else None,
        )

    def query_sum(d):
        zf = zl_of(d)
        j = zf * 2 + xs

        @pl.when(home)
        def _():
            for s in range(3):
                got(rb.at[s, zf], s_r.at[s, zf])
            total = (dqp[j].astype(F32) + rb[0, zf].astype(F32)) + (
                rb[1, zf].astype(F32) + rb[2, zf].astype(F32)
            )
            dqp[j] = total.astype(BF16)
            if d == 0:
                pltpu.make_async_copy(dqp.at[j, span(c)], oq_ref.at[span(zl)], s_own.at[1]).start()

        if d == 0:
            send(dqp.at[j, span(oc)], oq_ref.at[span(zl)], s_a.at[zl], partner, when=home)
        else:
            for r in (0, 1):
                send(dqp.at[j, span(r)], oq_ref.at[span(zl)], s_a.at[zl], dev(zl_to=zf, core=r), when=home)

    far = 1 - xs
    weigh(0)
    weigh(3)
    weights_of(0)
    key_part(4)
    b_pass(4)
    weigh(1)
    weights_of(3)
    key_part(3)
    weigh(2)
    weights_of(1)
    key_part(-3)
    weights_of(2)
    for d in (0, 3, 1, 2):
        turn(d)
    query_part(3, far)
    query_part(3, xs)
    y_pass(4)
    key_part(2)
    query_part(2, far)
    query_part(2, xs)
    b_pass(3)
    b_pass(-3)
    y_pass(3)
    key_part(-2)
    query_part(1, far)
    query_part(1, xs)
    y_pass(-3)
    key_part(1)
    query_part(0, far)
    query_part(0, xs)
    key_part(-1)
    a_pass(4)
    y_pass(2)
    key_part(0)
    b_pass(2)
    b_pass(-2)
    y_pass(-2)
    a_pass(3)
    a_pass(-3)
    y_pass(1)
    b_pass(1)
    b_pass(-1)
    query_sum(3)
    a_pass(2)
    a_pass(-2)
    y_pass(0)
    y_pass(-1)
    query_sum(2)
    for way in (0, 1):
        got(zb.at[way, 0], s_zb.at[way, 0])
    rest = dkp[0, pl.ds(a, b)].astype(F32) + (zb[0, 0].astype(F32) + zb[1, 0].astype(F32))
    dkp[0, pl.ds(a, b)] = rest.astype(BF16)
    for dy in (1, 3, 2):
        to = span(lax.rem(y + dy, 4))
        send(dkp.at[0, pl.ds(a, b), to], yb2.at[3 - dy], s_y2.at[3 - dy], dev(dy=dy))
    query_sum(1)
    a_pass(1)
    a_pass(-1)
    query_sum(0)
    total = a_sum(0)
    for s in range(3):
        got(yb2.at[s], s_y2.at[s])
    ok_ref[pl.ds(a, b), :] = (dkp[0, pl.ds(a, b), ycols].astype(F32) + yb2[0].astype(F32)) + (
        yb2[1].astype(F32) + yb2[2].astype(F32)
    )
    for d in (2, 1, 3):
        src = lax.rem(zl + d, 4)
        got(oq_ref.at[span(src)], s_a.at[src])
    mine = oq_ref.at[span(zl)]
    pl.when(away)(lambda: got(mine, s_a.at[zl]))
    pl.when(home)(lambda: pltpu.make_async_copy(mine, mine, s_own.at[1]).wait())

    for way in (0, 1):
        got(za.at[way, 0], s_za.at[way, 0])
    drain()
    ok_ref[pl.ds(0, a), :] = total + (za[0, 0].astype(F32) + za[1, 0].astype(F32))


def widen(q_ref, k_ref, oq_ref, ok_ref):
    oq_ref[...] = q_ref[...].astype(F32)
    ok_ref[...] = k_ref[...]


def on_device(queries, keys, query_ids, memory_ids, target_gap, lse, counts):
    a = ZFIRST
    b = BLK - a
    vmem = pl.BlockSpec(memory_space=pltpu.VMEM)
    hbm = pl.BlockSpec(memory_space=pl.ANY)
    dma = pltpu.SemaphoreType.DMA
    query_grad, key_grad = pl.pallas_call(
        kernel,
        out_shape=(
            jax.ShapeDtypeStruct((1024, BLK), BF16),
            jax.ShapeDtypeStruct((BLK, BLK), F32),
        ),
        in_specs=[hbm] * 2 + [vmem] * 5,
        out_specs=(hbm, vmem),
        scratch_shapes=[
            pltpu.VMEM((512, 2048), BF16),
            pltpu.VMEM((8, BLK, 1024), BF16),
            pltpu.VMEM((4, BLK, BLK), F32),
            pltpu.VMEM((4, 2, BLK, BLK), F32),
            pltpu.VMEM((4, BLK, BLK), F32),
            pltpu.VMEM((4, 8, BLK), jnp.int32),
            pltpu.VMEM((4, 8, BLK), F32),
            pltpu.VMEM((4, BLK, 512), BF16),
            pltpu.VMEM((512, 1024), BF16),
            pltpu.VMEM((8, BLK, 1024), BF16),
            pltpu.VMEM((8, 3, a, BLK), BF16),
            pltpu.VMEM((3, b, BLK), BF16),
            pltpu.VMEM((2, 4, a, BLK), BF16),
            pltpu.VMEM((2, 4, b, 1024), BF16),
            pltpu.VMEM((8, 512, BLK), BF16),
            pltpu.VMEM((3, 4, 512, BLK), BF16),
            dma((N_SENDS,)),
            dma((2,)),
            dma((9,)),
            dma((8, 4)),
            dma((9,)),
            dma((3,)),
            dma((8, 2)),
            dma((3,)),
            dma((4,)),
            dma((3,)),
            dma((4,)),
            dma((8, 4)),
            dma((3,)),
            dma((2, 4)),
            dma((2, 4)),
            dma((3, 4)),
            dma((4,)),
        ],
        compiler_params=pltpu.CompilerParams(
            collective_id=0, has_side_effects=True, vmem_limit_bytes=56 * 2**20
        ),
        cost_estimate=pl.CostEstimate(
            flops=6_442_450_944, bytes_accessed=3_000_000, transcendentals=262_144
        ),
        name="contrastive_backward",
    )(
        queries,
        keys,
        query_ids.reshape(1, -1),
        memory_ids.reshape(1, -1),
        target_gap.reshape(1, -1),
        lse.reshape(1, -1),
        counts.reshape(1, -1),
    )
    return pl.pallas_call(
        widen,
        out_shape=(
            jax.ShapeDtypeStruct((1024, BLK), F32),
            jax.ShapeDtypeStruct((BLK, BLK), F32),
        ),
        in_specs=[vmem] * 2,
        out_specs=(vmem, vmem),
        cost_estimate=pl.CostEstimate(flops=0, bytes_accessed=2_097_152, transcendentals=0),
        name="widen",
    )(query_grad, key_grad)


def solution(mesh):
    torus = Mesh(mesh.devices.reshape(2, 4, 2, 4, 4), AXES)
    return jax.shard_map(
        on_device,
        mesh=torus,
        in_specs=(P(PB, MA), P(MA, PB), P(PB), P(MA), P(PB), P(PB), P(PB)),
        out_specs=(P(PB, MA), P(MA, PB)),
        check_vma=False,
    )
```

```python
import math

import jax
import jax.numpy as jnp
from jax import lax
from jax.experimental import pallas as pl
from jax.experimental.pallas import tpu as pltpu
from jax.sharding import Mesh
from jax.sharding import PartitionSpec as P

D = 4096
GRAD_SCALE = 1024
AXES = ("zh", "y", "core", "zl", "x")
PB = ("zh", "y", "core")
MA = ("zl", "x")
FACTOR = 1.0 / math.sqrt(D)
BLK = 256
ZFIRST = 192
F32 = jnp.float32
BF16 = jnp.bfloat16
OFFSETS = (0, 1, -1, 2, -2, 3, -3, 4)
RANK = {dz: i for i, dz in enumerate(OFFSETS)}
N_SENDS = 89


def nt(a, b):
    return lax.dot_general(a, b, (((1,), (1,)), ((), ())), preferred_element_type=F32)


def nn(a, b):
    return jnp.dot(a, b, preferred_element_type=F32)


def kernel(
    q_ref, k_ref, qid_ref, mid_ref, gap_ref, lse_ref, cnt_ref, oq_ref, ok_ref,
    qb, kb, mk, st, sx, idb, mb, wt, wn, dkp, yb, yb2, za, zb, dqp, rb,
    ssem, s_own, s_kz, s_ky, s_bz, s_by, s_q, s_id, s_sx, s_m, s_w, s_y, s_y2, s_za, s_zb, s_r, s_a,
):
    zh, y, c, zl, x = [lax.axis_index(a) for a in AXES]
    z = zh * 4 + zl
    xp = lax.rem(x, 2)
    xs = x // 2
    home = xp == c
    oc = 1 - c
    a = ZFIRST
    ah = a // 2
    b = BLK - a
    bh = b // 2

    def zat(dz):
        return lax.rem(z + dz + 8, 8)

    def dev(dx=0, dy=0, dz=0, core=None, zl_to=None, x_to=None):
        zz = zat(dz)
        return (
            zz // 4,
            lax.rem(y + dy, 4),
            c if core is None else core,
            lax.rem(zz, 4) if zl_to is None else zl_to,
            lax.rem(x + dx, 4) if x_to is None else x_to,
        )

    def span(i, n=BLK):
        return pl.ds(pl.multiple_of(i * n, n), n)

    sends = []

    def send(src, dst, recv, to, when=None):
        copy = pltpu.make_async_remote_copy(
            src_ref=src,
            dst_ref=dst,
            send_sem=ssem.at[len(sends)],
            recv_sem=recv,
            device_id=to,
            device_id_type=pl.DeviceIdType.MESH,
        )
        if when is None:
            copy.start()
        else:
            pl.when(when)(copy.start)
        sends.append((copy, when))

    def drain():
        groups = {}
        for copy, when in sends:
            groups.setdefault(id(when), (when, []))[1].append(copy)
        for when, copies in groups.values():

            def wait_all(copies=copies):
                for copy in copies:
                    copy.wait_send()

            if when is None:
                wait_all()
            else:
                pl.when(when)(wait_all)
        sends.clear()

    partner = dev(core=oc)
    away = jnp.logical_not(home)

    def got(dst, recv):
        pltpu.make_async_remote_copy(
            src_ref=dst,
            dst_ref=dst,
            send_sem=ssem.at[0],
            recv_sem=recv,
            device_id=partner,
            device_id_type=pl.DeviceIdType.MESH,
        ).wait_recv()

    barrier = pltpu.get_barrier_semaphore()
    peers = [partner, dev(dz=1), dev(dz=-1)]
    for d in (1, 2, 3):
        other = lax.rem(zl + d, 4)
        peers += [dev(dx=d), dev(dy=d), dev(zl_to=other), dev(zl_to=other, core=oc)]
    for peer in peers:
        pl.semaphore_signal(barrier, inc=1, device_id=peer, device_id_type=pl.DeviceIdType.MESH)
    ycols = span(y)
    own_keys = pltpu.make_async_copy(k_ref, kb.at[z, :, ycols], s_own.at[0])
    own_keys.start()
    idb[zl] = jnp.broadcast_to(mid_ref[...], (8, BLK))
    pl.semaphore_wait(barrier, len(peers))

    def zslot(dz):
        return kb.at[zat(dz)]

    def a_block(dz, dy, rows):
        return kb.at[zat(dz), rows, span(lax.rem(y + dy, 4))]

    def a_z(dz, step, rows, part):
        blk = a_block(dz, 0, rows)
        to = dz - step
        i = 8 if part == 1 else RANK[4 if to == -4 else to]
        send(k_ref.at[rows] if dz == 0 else blk, blk, s_kz.at[i], dev(dz=step))

    def a_y(dz):
        blk = a_block(dz, 0, pl.ds(0, a))
        for dy in (1, 3):
            send(k_ref.at[pl.ds(0, a)] if dz == 0 else blk, blk, s_ky.at[RANK[dz], 3 - dy], dev(dy=dy))

    def a_relay(*offsets):
        for dz in offsets:
            i = RANK[dz]
            got(a_block(dz, 3, pl.ds(0, a)), s_ky.at[i, 2])
            blk = a_block(dz, 3, pl.ds(0, ah))
            send(blk, blk, s_ky.at[i, 1], dev(dy=1))
            got(a_block(dz, 1, pl.ds(0, a)), s_ky.at[i, 0])
            blk = a_block(dz, 1, pl.ds(ah, ah))
            send(blk, blk, s_ky.at[i, 3], dev(dy=3))

    def a_arrive(dz):
        for sign in (-1, 1) if dz < 4 else (0,):
            if dz == 4:
                got(a_block(4, 0, pl.ds(0, ah)), s_kz.at[7])
                got(a_block(4, 0, pl.ds(ah, ah)), s_kz.at[8])
                a_y(4)
                continue
            at = sign * dz
            got(a_block(at, 0, pl.ds(0, a)), s_kz.at[RANK[at]])
            if dz < 3:
                a_z(at, -sign, pl.ds(0, a), 0)
            elif sign < 0:
                a_z(at, 1, pl.ds(0, ah), 0)
            else:
                a_z(at, -1, pl.ds(ah, ah), 1)
        if dz < 4:
            a_y(-dz)
            a_y(dz)

    def b_z(dz, step, rows, part):
        blk = kb.at[zat(dz), rows]
        to = dz - step
        i = 8 if part == 1 else RANK[4 if to == -4 else to]
        send(blk, blk, s_bz.at[i], dev(dz=step))

    def b_arrive(dz):
        for sign in (-1, 1):
            at = sign * dz
            got(kb.at[zat(at), pl.ds(a, b)], s_bz.at[RANK[at]])
            if dz < 3:
                b_z(at, -sign, pl.ds(a, b), 0)
            elif sign < 0:
                b_z(at, 1, pl.ds(a, bh), 0)
            else:
                b_z(at, -1, pl.ds(a + bh, bh), 1)

    def q_block(j, r):
        return qb.at[span(r), span(j)]

    def zl_of(d):
        return (zl, zl + 1 - 2 * lax.rem(zl, 2), lax.rem(zl + 2, 4), 3 - zl)[d]

    j_own = zl * 2 + xs
    for d in (1, 2, 3):
        send(idb.at[zl], idb.at[zl], s_id.at[3 - d], dev(zl_to=lax.rem(zl + d, 4)))
    send(q_ref.at[span(zl)], q_block(j_own, c), s_q.at[j_own, c], dev(core=xp), when=away)

    def q_exchange(d):
        to = zl_of(d)
        send(q_ref.at[span(to)], q_block(j_own, c), s_q.at[j_own, c], dev(zl_to=to, core=xp))

    own_queries = pltpu.make_async_copy(q_ref.at[span(zl)], q_block(j_own, c), s_own.at[1])
    pl.when(home)(own_queries.start)

    def q_spread(j, r, own=False):
        if not own:
            pl.when(home)(lambda: got(q_block(j, r), s_q.at[j, r]))
        src = q_ref.at[span(zl)] if own else q_block(j, r)
        for dx in (1, 3):
            send(src, q_block(j, r), s_q.at[j, r], dev(dx=dx), when=home)

    def q_arrive(d):
        j = zl_of(d) * 2 + xs
        q_spread(j, 0)
        q_spread(j, 1)

    def q_from(dx, d):
        return zl_of(d) * 2 + lax.rem(x + dx, 4) // 2

    def q_relay(d):
        for r, dx in ((0, 3), (1, 1)):
            blk = q_block(q_from(dx, d), r)
            sem = s_q.at[q_from(dx, d), r]
            pl.when(away)(lambda: got(blk, sem))
            send(blk, blk, sem, dev(dx=4 - dx), when=away)

    qrow = span(zl)
    qid = qid_ref[:, qrow].astype(F32)
    lse = lse_ref[:, qrow]

    def matches():
        for d in (0, 1, 2, 3):
            m = lax.rem(zl + d, 4)
            if d > 0:
                got(idb.at[m], s_id.at[d - 1])
            ids = jnp.broadcast_to(idb[m][0:1, :].astype(F32), (128, BLK)).T
            mk[m] = (ids[:, 0:1] == qid).astype(F32)

    def scores(dz, last):
        i = RANK[dz]
        got(a_block(dz, 2, pl.ds(0, ah)), s_ky.at[i, 1])
        got(a_block(dz, 2, pl.ds(ah, ah)), s_ky.at[i, 3])
        if dz == 4:
            got(kb.at[zat(4), pl.ds(a, bh)], s_bz.at[7])
            got(kb.at[zat(4), pl.ds(a + bh, bh)], s_bz.at[8])
        m = lax.rem(zat(dz), 4)
        part = zat(dz) // 4
        for r in (oc, c):
            s = nt(kb[zat(dz)], qb[span(r), span(part, 1024)])
            st[m, r] = st[m, r] + s if last else s
            if last and r is oc:
                send(st.at[m, oc], sx.at[m], s_sx.at[m], partner)

    def probs(dz):
        m = lax.rem(zat(dz), 4)
        got(sx.at[m], s_sx.at[m])
        p = jnp.exp((st[m, c] + sx[m]) * FACTOR - lse)
        st[m, c] = p
        return jnp.sum(mk[m] * p, axis=0, keepdims=True)

    a_z(0, 1, pl.ds(0, a), 0)
    a_z(0, -1, pl.ds(0, a), 0)
    a_y(0)
    q_spread(j_own, c, own=True)
    q_spread(j_own, oc)
    pl.when(home)(own_queries.wait)
    q_exchange(3)
    for dy in (1, 3, 2):
        send(k_ref.at[pl.ds(a, b)], a_block(0, 0, pl.ds(a, b)), s_by.at[3 - dy], dev(dy=dy))
    a_arrive(1)
    q_exchange(1)
    q_exchange(2)
    a_relay(0)
    a_relay(1)
    own_keys.wait()
    for dy in (1, 3, 2):
        got(a_block(0, 4 - dy, pl.ds(a, b)), s_by.at[3 - dy])
    b_z(0, 1, pl.ds(a, b), 0)
    b_z(0, -1, pl.ds(a, b), 0)
    q_relay(0)
    q_arrive(3)
    q_arrive(1)
    a_arrive(2)
    q_arrive(2)
    matches()
    b_arrive(1)
    q_relay(1)
    a_relay(-1)
    a_arrive(3)
    b_arrive(2)
    a_arrive(4)
    a_relay(2)
    q_relay(3)
    q_relay(2)
    b_arrive(3)
    a_relay(-2)
    a_relay(3)
    a_relay(-3)
    @pl.when(home)
    def _():
        for d in (0, 1, 2, 3):
            for r in (0, 1):
                j = zl_of(d) * 2 + (1 - xs)
                got(q_block(j, r), s_q.at[j, r])

    @pl.when(away)
    def _():
        for d in (0, 1, 2, 3):
            for r, dx in ((1, 3), (0, 1)):
                j = q_from(dx, d)
                got(q_block(j, r), s_q.at[j, r])

    scores(0, False)
    scores(1, False)
    a_relay(4)
    scores(-1, False)
    scores(2, False)
    scores(-2, True)
    scores(3, True)
    matched = probs(-2)
    scores(-3, True)
    matched = matched + probs(3)
    scores(4, True)
    matched = matched + probs(-3)
    matched = matched + probs(4)

    mb[0] = jnp.broadcast_to(matched, (8, BLK))
    for d in (1, 3, 2):
        send(mb.at[0], mb.at[4 - d], s_m.at[3 - d], dev(dx=d))
    scale = jnp.float32(GRAD_SCALE) / cnt_ref[:, qrow].astype(F32)
    gap = jnp.exp(gap_ref[:, qrow])
    drain()
    for d in (1, 3, 2):
        got(mb.at[4 - d], s_m.at[3 - d])
    positive = gap + ((mb[0] + mb[1]) + (mb[2] + mb[3]))[0:1, :]
    inverse = 1.0 / positive

    def weigh(d):
        m = lax.rem(zl + d, 4)
        p = st[m, c]
        st[m, c] = (p - mk[m] * p * inverse) * scale
        wt[m, :, span(c)] = st[m, c].astype(BF16)
        blk = wt.at[m, :, span(c)]
        send(blk, blk, s_w.at[m], partner)

    def weights_of(d):
        m = lax.rem(zl + d, 4)
        got(wt.at[m, :, span(oc)], s_w.at[m])

    def turn(d):
        m = lax.rem(zl + d, 4)
        wn[span(c), span(m)] = st[m, c].T.astype(BF16)
        wn[span(oc), span(m)] = wt[m, :, span(oc)].astype(F32).T.astype(BF16)

    def key_part(dz):
        i = RANK[dz]
        m = lax.rem(zat(dz), 4)
        part = zat(dz) // 4
        dkp[i] = (nn(wt[m], qb[:, span(part, 1024)]) * FACTOR).astype(BF16)
        far = span(lax.rem(y + 2, 4))
        for way, rows in ((0, pl.ds(0, ah)), (1, pl.ds(ah, ah))):
            send(dkp.at[i, rows, far], yb.at[i, 2, rows], s_y.at[i, 2 + way], dev(dy=1 + 2 * way))

    def y_pass(*offsets):
        for dz in offsets:
            i = RANK[dz]
            for way, rows in ((0, pl.ds(0, ah)), (1, pl.ds(ah, ah))):
                dy = 1 + 2 * way
                to = span(lax.rem(y + dy, 4))
                got(yb.at[i, 2, rows], s_y.at[i, 2 + way])
                dkp[i, rows, to] = (dkp[i, rows, to].astype(F32) + yb[i, 2, rows].astype(F32)).astype(BF16)
                send(dkp.at[i, pl.ds(0, a), to], yb.at[i, way], s_y.at[i, way], dev(dy=dy))

    def chain(dz, buf, sem, half):
        way = 0 if dz > 0 else 1
        left = abs(dz)
        if left == 3:
            rows = pl.ds(0, half) if dz > 0 else pl.ds(half, half)
        else:
            rows = pl.ds(0, 2 * half)
        got(buf.at[way, left, rows], sem.at[way, left])
        return way, left, rows

    def a_sum(dz):
        i = RANK[dz]
        for s in range(2):
            got(yb.at[i, s], s_y.at[i, s])
        return dkp[i, pl.ds(0, a), ycols].astype(F32) + (yb[i, 0].astype(F32) + yb[i, 1].astype(F32))

    def a_pass(dz):
        i = RANK[dz]
        dkp[i, pl.ds(0, a), ycols] = a_sum(dz).astype(BF16)
        if dz == 4:
            for way, rows in ((0, pl.ds(0, ah)), (1, pl.ds(ah, ah))):
                send(dkp.at[i, rows, ycols], za.at[way, 3, rows], s_za.at[way, 3], dev(dz=1 - 2 * way))
            return
        way, left, rows = chain(dz, za, s_za, ah)
        mine = dkp[i, rows, ycols].astype(F32) + za[way, left, rows].astype(F32)
        dkp[i, rows, ycols] = mine.astype(BF16)
        send(dkp.at[i, pl.ds(0, a), ycols], za.at[way, left - 1], s_za.at[way, left - 1], dev(dz=1 - 2 * way))

    def b_pass(dz):
        i = RANK[dz]
        if dz == 4:
            for way, rows in ((0, 0), (1, bh)):
                src = dkp.at[i, pl.ds(a + rows, bh)]
                send(src, zb.at[way, 3, pl.ds(rows, bh)], s_zb.at[way, 3], dev(dz=1 - 2 * way))
            return
        way, left, rows = chain(dz, zb, s_zb, bh)
        mine = pl.ds(a + rows.start, rows.size)
        dkp[i, mine] = (dkp[i, mine].astype(F32) + zb[way, left, rows].astype(F32)).astype(BF16)
        send(dkp.at[i, pl.ds(a, b)], zb.at[way, left - 1], s_zb.at[way, left - 1], dev(dz=1 - 2 * way))

    def query_part(d, s):
        zf = zl_of(d)
        j = zf * 2 + s
        keys = kb[pl.ds(pl.multiple_of((zf // 2) * 4, 4), 4), :, span(lax.rem(j, 4))]
        dqp[j] = (nn(wn[...], keys.reshape(1024, BLK)) * FACTOR).astype(BF16)
        to = 2 * s + c
        slot = lax.rem(x - to + 4, 4) - 1
        if s is xs:
            slot = jnp.maximum(slot, 0)
        send(
            dqp.at[j], rb.at[slot, zf], s_r.at[slot, zf], dev(x_to=to),
            when=away if s is xs else None,
        )

    def query_sum(d):
        zf = zl_of(d)
        j = zf * 2 + xs

        @pl.when(home)
        def _():
            for s in range(3):
                got(rb.at[s, zf], s_r.at[s, zf])
            total = (dqp[j].astype(F32) + rb[0, zf].astype(F32)) + (
                rb[1, zf].astype(F32) + rb[2, zf].astype(F32)
            )
            dqp[j] = total.astype(BF16)
            if d == 0:
                pltpu.make_async_copy(dqp.at[j, span(c)], oq_ref.at[span(zl)], s_own.at[1]).start()

        if d == 0:
            send(dqp.at[j, span(oc)], oq_ref.at[span(zl)], s_a.at[zl], partner, when=home)
        else:
            for r in (0, 1):
                send(dqp.at[j, span(r)], oq_ref.at[span(zl)], s_a.at[zl], dev(zl_to=zf, core=r), when=home)

    far = 1 - xs
    weigh(0)
    weigh(3)
    weigh(1)
    weights_of(0)
    key_part(4)
    b_pass(4)
    weights_of(3)
    key_part(3)
    weigh(2)
    weights_of(1)
    key_part(-3)
    weights_of(2)
    for d in (0, 3, 1, 2):
        turn(d)
    query_part(3, far)
    query_part(3, xs)
    y_pass(4)
    key_part(2)
    query_part(2, far)
    query_part(2, xs)
    b_pass(3)
    b_pass(-3)
    y_pass(3)
    key_part(-2)
    query_part(1, far)
    query_part(1, xs)
    y_pass(-3)
    key_part(1)
    query_part(0, far)
    query_part(0, xs)
    key_part(-1)
    a_pass(4)
    y_pass(2)
    key_part(0)
    b_pass(2)
    b_pass(-2)
    y_pass(-2)
    a_pass(3)
    a_pass(-3)
    y_pass(1)
    b_pass(1)
    b_pass(-1)
    query_sum(3)
    a_pass(2)
    a_pass(-2)
    y_pass(0)
    y_pass(-1)
    query_sum(2)
    for way in (0, 1):
        got(zb.at[way, 0], s_zb.at[way, 0])
    rest = dkp[0, pl.ds(a, b)].astype(F32) + (zb[0, 0].astype(F32) + zb[1, 0].astype(F32))
    dkp[0, pl.ds(a, b)] = rest.astype(BF16)
    for dy in (1, 3, 2):
        to = span(lax.rem(y + dy, 4))
        send(dkp.at[0, pl.ds(a, b), to], yb2.at[3 - dy], s_y2.at[3 - dy], dev(dy=dy))
    query_sum(1)
    a_pass(1)
    a_pass(-1)
    query_sum(0)
    total = a_sum(0)
    for s in range(3):
        got(yb2.at[s], s_y2.at[s])
    ok_ref[pl.ds(a, b), :] = (dkp[0, pl.ds(a, b), ycols].astype(F32) + yb2[0].astype(F32)) + (
        yb2[1].astype(F32) + yb2[2].astype(F32)
    )
    for d in (2, 1, 3):
        src = lax.rem(zl + d, 4)
        got(oq_ref.at[span(src)], s_a.at[src])
    mine = oq_ref.at[span(zl)]
    pl.when(away)(lambda: got(mine, s_a.at[zl]))
    pl.when(home)(lambda: pltpu.make_async_copy(mine, mine, s_own.at[1]).wait())

    for way in (0, 1):
        got(za.at[way, 0], s_za.at[way, 0])
    drain()
    ok_ref[pl.ds(0, a), :] = total + (za[0, 0].astype(F32) + za[1, 0].astype(F32))


def widen(q_ref, k_ref, oq_ref, ok_ref):
    oq_ref[...] = q_ref[...].astype(F32)
    ok_ref[...] = k_ref[...]


def on_device(queries, keys, query_ids, memory_ids, target_gap, lse, counts):
    a = ZFIRST
    b = BLK - a
    vmem = pl.BlockSpec(memory_space=pltpu.VMEM)
    hbm = pl.BlockSpec(memory_space=pl.ANY)
    dma = pltpu.SemaphoreType.DMA
    query_grad, key_grad = pl.pallas_call(
        kernel,
        out_shape=(
            jax.ShapeDtypeStruct((1024, BLK), BF16),
            jax.ShapeDtypeStruct((BLK, BLK), F32),
        ),
        in_specs=[hbm] * 2 + [vmem] * 5,
        out_specs=(hbm, vmem),
        scratch_shapes=[
            pltpu.VMEM((512, 2048), BF16),
            pltpu.VMEM((8, BLK, 1024), BF16),
            pltpu.VMEM((4, BLK, BLK), F32),
            pltpu.VMEM((4, 2, BLK, BLK), F32),
            pltpu.VMEM((4, BLK, BLK), F32),
            pltpu.VMEM((4, 8, BLK), jnp.int32),
            pltpu.VMEM((4, 8, BLK), F32),
            pltpu.VMEM((4, BLK, 512), BF16),
            pltpu.VMEM((512, 1024), BF16),
            pltpu.VMEM((8, BLK, 1024), BF16),
            pltpu.VMEM((8, 3, a, BLK), BF16),
            pltpu.VMEM((3, b, BLK), BF16),
            pltpu.VMEM((2, 4, a, BLK), BF16),
            pltpu.VMEM((2, 4, b, 1024), BF16),
            pltpu.VMEM((8, 512, BLK), BF16),
            pltpu.VMEM((3, 4, 512, BLK), BF16),
            dma((N_SENDS,)),
            dma((2,)),
            dma((9,)),
            dma((8, 4)),
            dma((9,)),
            dma((3,)),
            dma((8, 2)),
            dma((3,)),
            dma((4,)),
            dma((3,)),
            dma((4,)),
            dma((8, 4)),
            dma((3,)),
            dma((2, 4)),
            dma((2, 4)),
            dma((3, 4)),
            dma((4,)),
        ],
        compiler_params=pltpu.CompilerParams(
            collective_id=0, has_side_effects=True, vmem_limit_bytes=56 * 2**20
        ),
        cost_estimate=pl.CostEstimate(
            flops=6_442_450_944, bytes_accessed=3_000_000, transcendentals=262_144
        ),
        name="contrastive_backward",
    )(
        queries,
        keys,
        query_ids.reshape(1, -1),
        memory_ids.reshape(1, -1),
        target_gap.reshape(1, -1),
        lse.reshape(1, -1),
        counts.reshape(1, -1),
    )
    return pl.pallas_call(
        widen,
        out_shape=(
            jax.ShapeDtypeStruct((1024, BLK), F32),
            jax.ShapeDtypeStruct((BLK, BLK), F32),
        ),
        in_specs=[vmem] * 2,
        out_specs=(vmem, vmem),
        cost_estimate=pl.CostEstimate(flops=0, bytes_accessed=2_097_152, transcendentals=0),
        name="widen",
    )(query_grad, key_grad)


def solution(mesh):
    torus = Mesh(mesh.devices.reshape(2, 4, 2, 4, 4), AXES)
    return jax.shard_map(
        on_device,
        mesh=torus,
        in_specs=(P(PB, MA), P(MA, PB), P(PB), P(MA), P(PB), P(PB), P(PB)),
        out_specs=(P(PB, MA), P(MA, PB)),
        check_vma=False,
    )
```
